512 devices in a mesh: dom: 64 (over x, z), sub: 8 (over y, core).
Axes of the slice: x: 4, y: 4, z: 16, core: 2. Of those that a mesh axis runs over, the one named last changes fastest.
Arguments:
- right_side: float32 [1024, 16, 128], P(('dom', 'sub')), as said below
- diag_blocks: float32 [1024, 128, 128], P(('dom', 'sub')), as said below
- block_values: float32 [1024, 4, 128, 128], P(('dom', 'sub')), as said below
- block_cols: int32 [1024, 4], P(('dom', 'sub')), may hold values from 0 to 31, as said below
- block_count: int32 [1024], P(('dom', 'sub')), may hold values from 0 to 4, as said below
- cell_diagonal: float32 [1024, 128], P(('dom', 'sub')), as said below
Outputs:
- solution_field: float32 [1024, 16, 128], P(('dom', 'sub'))
- residual: float32 [1024, 16, 128], P(('dom', 'sub'))
The draws below stay inside these ranges and needn't reach their ends.
Inputs may be any that keep to these rules, and one draw needn't show every extreme that they name: `block_cols`: live slots of a block row point to distinct block rows that come after it in the window (positions 0 to 15 are the block rows of the same index of dom, the rest those of the next index); block rows of the last index of dom point only into their own index; dead slots hold 0. `block_count`: the number of live slots, which varies from device to device. `block_values`: entries lie between -1 / 128 and 0. `diag_blocks`: entries lie between -1 / 128 and 0. `cell_diagonal`: every entry exceeds 1 + the live slots of its block row + the live slots of all block rows that couple to its block row, so the operator is strictly diagonally dominant. `right_side`: entries lie between -50 and 50.
All inputs are finite; a program needn't handle non-finite values.
Results may differ from the reference program's by a relative error of at most 0.00065.
Values sent between devices are 32-bit elements; how exact they have to be, the bound alone decides.
A program may use at most 64 MiB of HBM per device.

```python
import jax
import jax.numpy as jnp
from jax import lax

BS = 128
K = 4
NRHS = 16
ITERS = 3
R = 2
NB = 1024
WIN = 32
N_DOM = 64


def pattern(key):
    key_first, key_second, key_third = jax.random.split(key, 3)
    half_win = WIN // 2
    row_ids = jnp.arange(NB, dtype=jnp.int32)
    group_index = row_ids // half_win
    position = row_ids % half_win
    window_limit = jnp.where(group_index == N_DOM - 1, half_win, WIN)
    window_spots = jnp.arange(WIN, dtype=jnp.int32)
    usable = (window_spots[None, :] > position[:, None]) & (window_spots[None, :] < window_limit[:, None])
    noise_ints = jax.random.randint(key_first, (NB, WIN), 1, 1 << 16)
    scores = jnp.where(usable, noise_ints * WIN + window_spots[None, :] + 1, 0)
    forced = (row_ids[:, None] == 0) & (window_spots[None, :] == WIN - 1)
    scores = jnp.where(forced, (1 << 16) * WIN + WIN + 1, scores)
    top_scores, picked = lax.top_k(scores, K)
    available = jnp.sum(usable.astype(jnp.int32), axis=1)
    device_ids = row_ids // R
    device_level = jax.random.randint(key_second, (NB // R,), 1, K + 1)[device_ids]
    wanted = jnp.minimum(jax.random.randint(key_third, (NB,), 1, K + 1), device_level)
    wanted = jnp.where(row_ids == 0, K, wanted)
    live_count = jnp.minimum(wanted, available).astype(jnp.int32)
    slot_ids = jnp.arange(K, dtype=jnp.int32)
    live_slots = slot_ids[None, :] < live_count[:, None]
    columns = jnp.where(live_slots, picked, 0).astype(jnp.int32)
    targets = jnp.where(live_slots, group_index[:, None] * half_win + columns, row_ids[:, None])
    indegree = jax.ops.segment_sum(live_slots.astype(jnp.int32).reshape(NB * K), targets.reshape(NB * K), num_segments=NB)
    return (columns, live_count, indegree.astype(jnp.int32))


def draw_block_cols(key, part):
    return pattern(key)[0]


def draw_block_count(key, part):
    return pattern(key)[1]


def draw_cell_diagonal(key, part):
    columns, live_count, indegree = pattern(key)
    key = jax.random.fold_in(key, 11)
    extra = jnp.exp(jax.random.uniform(key, (NB, BS), jnp.float32, jnp.log(0.3), jnp.log(3.0)))
    bound = (1 + live_count + indegree).astype(jnp.float32)
    return bound[:, None] + extra


def draw_block_values(key, part):
    key = jax.random.fold_in(key, 7)
    spread_vals = jax.random.uniform(key, (NB, K, BS, BS), jnp.float32, 0.0, 1.0)
    return -spread_vals / BS


def draw_diag_blocks(key, part):
    key = jax.random.fold_in(key, 9)
    spread_vals = jax.random.uniform(key, (NB, BS, BS), jnp.float32, 0.0, 1.0)
    return -spread_vals / BS


def draw_right_side(key, part):
    key = jax.random.fold_in(key, 5)
    key_first = jax.random.fold_in(key, 0)
    row_ids = jnp.arange(NB, dtype=jnp.int32).astype(jnp.float32)
    rise_factor = (1.0 + 2.0 * (row_ids + 0.5) / NB)[:, None, None]
    base_values = jnp.clip(jax.random.normal(key_first, (NB, NRHS, BS), jnp.float32), -6.0, 6.0)
    return (base_values + 0.5) * rise_factor


def setup_inputs(seed: int = 0) -> dict:
    splits = jax.random.split(jax.random.key(seed), 7)
    right_side = draw_right_side(jax.random.fold_in(splits[6], 71), 0)
    diag_blocks = draw_diag_blocks(jax.random.fold_in(splits[6], 71), 0)
    block_values = draw_block_values(jax.random.fold_in(splits[6], 71), 0)
    block_cols = draw_block_cols(jax.random.fold_in(splits[6], 71), 0)
    block_count = draw_block_count(jax.random.fold_in(splits[6], 71), 0)
    cell_diagonal = draw_cell_diagonal(jax.random.fold_in(splits[6], 71), 0)
    return {"right_side": right_side, "diag_blocks": diag_blocks, "block_values": block_values, "block_cols": block_cols, "block_count": block_count, "cell_diagonal": cell_diagonal}


PRECISE = lax.Precision.HIGHEST


def operator_apply(vector, diag_blocks, block_values, block_cols, block_count, cell_diagonal):
    upper_part = jnp.triu(diag_blocks, 1)
    own_part = jnp.einsum('rab,rzb->rza', upper_part, vector, precision=PRECISE)
    own_part = own_part + jnp.einsum('rba,rzb->rza', upper_part, vector, precision=PRECISE)
    own_part = own_part + cell_diagonal[:, None, :] * vector
    row_ids = jnp.arange(NB, dtype=jnp.int32)
    window_base = (row_ids // (WIN // 2)) * (WIN // 2)
    live_slots = jnp.arange(K, dtype=jnp.int32)[None, :] < block_count[:, None]
    targets = jnp.where(live_slots, window_base[:, None] + block_cols, row_ids[:, None]).astype(jnp.int32)
    weights = live_slots.astype(jnp.float32)
    far_rows = vector[targets] * weights[:, :, None, None]
    forward = jnp.einsum('rkab,rkzb->rza', block_values, far_rows, precision=PRECISE)
    back_terms = jnp.einsum('rkba,rzb->rkza', block_values, vector, precision=PRECISE) * weights[:, :, None, None]
    back_sum = jax.ops.segment_sum(back_terms.reshape(NB * K, NRHS, BS), targets.reshape(NB * K), num_segments=NB)
    return own_part + forward + back_sum


def global_dots(first, second):
    return jnp.sum(first * second, axis=(0, 2))


def reference(right_side, diag_blocks, block_values, block_cols, block_count, cell_diagonal):
    solution_field = jnp.zeros_like(right_side)
    residual = right_side
    precond_res = residual / cell_diagonal[:, None, :]
    direction = precond_res
    precond_dot = global_dots(residual, precond_res)
    for iteration in range(ITERS):
        image_vec = operator_apply(direction, diag_blocks, block_values, block_cols, block_count, cell_diagonal)
        step_size = precond_dot / global_dots(direction, image_vec)
        solution_field = solution_field + step_size[None, :, None] * direction
        residual = residual - step_size[None, :, None] * image_vec
        precond_res = residual / cell_diagonal[:, None, :]
        new_dot = global_dots(residual, precond_res)
        direction = precond_res + (new_dot / precond_dot)[None, :, None] * direction
        precond_dot = new_dot
    return solution_field, residual
```

```python
import functools

import jax
import jax.numpy as jnp
from jax import lax
from jax.experimental import pallas as pl
from jax.experimental.pallas import tpu as pltpu
from jax.sharding import PartitionSpec as P

MESH = pl.DeviceIdType.MESH
K = 4
ITERS = 3
BS = 128
HALF = 8
X, Y, Z = 4, 4, 16
N_DOM = X * Z
GROUP = 4 * Y
F32, BF16, I32 = jnp.float32, jnp.bfloat16, jnp.int32


def ring_order(n):
    return sorted(range(1, n), key=lambda d: -min(d, n - d))


def split(v):
    high = v.astype(BF16).astype(F32)
    return jnp.concatenate([high, v - high], axis=0).astype(BF16)


def kernel(
    right_ref, diag_ref, blocks_ref, cols_ref, count_ref, celld_ref,
    x_out, res_out,
    rhs, dst, diag_in, dcell, sym, blocks, table_v, table_w, place_s, slot_s, w_off, w_sym,
    mine, win_0, win_1, win_2, prods, spread, tin, red_src, red_a, red_b, outs,
    local_sems, pair_send, pair_recv, ex_send, ex_recv, red_send, red_recv,
):
    dom, sub = lax.axis_index("dom"), lax.axis_index("sub")
    xx, zz = dom // Z, lax.rem(dom, Z)
    yy, core = sub // 2, lax.rem(sub, 2)
    other = 1 - core
    own = pl.ds(2 * core, 2)
    theirs = pl.ds(2 * other, 2)
    partner = (dom, 2 * yy + other)

    def at(dx, dy, dz):
        return (
            lax.rem(xx + dx, X) * Z + lax.rem(zz + dz, Z),
            2 * lax.rem(yy + dy, Y) + core,
        )

    def dom_at(step, dy):
        return (lax.rem(dom + step + N_DOM, N_DOM), 2 * lax.rem(yy + dy, Y) + core)

    loads = [
        pltpu.make_async_copy(celld_ref, dcell, local_sems.at[0]),
        pltpu.make_async_copy(right_ref.at[:, pl.ds(HALF * core, HALF)], rhs.at[own], local_sems.at[1]),
        pltpu.make_async_copy(diag_ref, diag_in, local_sems.at[2]),
        pltpu.make_async_copy(blocks_ref, blocks.at[own], local_sems.at[3]),
    ]
    for load in loads:
        load.start()

    win = (win_0, win_1, win_2)
    for window in win:
        window[...] = jnp.zeros_like(window)
    tin[...] = jnp.zeros_like(tin)

    barrier = pltpu.get_barrier_semaphore()
    plane = [(dx, dy) for dx in range(X) for dy in range(Y) if dx or dy]
    plane.sort(key=lambda p: -(min(p[0], X - p[0]) + min(p[1], Y - p[1])))
    greet = [partner]
    greet += [at(0, 0, dz) for dz in ring_order(Z)]
    greet += [at(dx, dy, 0) for dx, dy in plane]
    greet += [dom_at(step, dy) for step in (1, -1) for dy in range(Y)]
    for device in greet:
        pl.semaphore_signal(barrier, inc=1, device_id=device, device_id_type=MESH)

    for h in range(4):
        prods[5 * h + K] = jnp.zeros((HALF, BS), F32)
    lane = lax.broadcasted_iota(I32, (1, BS), 1)
    places = []
    for i in range(2):
        row = jnp.zeros((1, BS), I32)
        for k in range(K):
            place = jnp.where(k < count_ref[i], cols_ref[i, k], 2 * GROUP)
            row = jnp.where(lane == k, place, row)
            places.append(place)
        table_v[i : i + 1, :] = row
    table_v[2:8, :] = jnp.zeros((6, BS), I32)

    def tabulate(base, places):
        for i in range(2):
            for k in range(K):
                place_s[(base + i) * K + k] = places[i * K + k]
            for w in range(2 * GROUP):
                slot = K
                for k in range(K):
                    slot = jnp.where(places[i * K + k] == w, k, slot)
                slot_s[(base + i) * 2 * GROUP + w] = slot + (base + i) * (K + 1)

    tabulate(2 * core, places)

    loads[0].wait()
    for i in range(2):
        dst[2 * core + i] = jnp.broadcast_to(dcell[i : i + 1, :], (HALF, BS))
    loads[2].wait()
    upper = lax.broadcasted_iota(I32, (BS, BS), 0) < lax.broadcasted_iota(I32, (BS, BS), 1)
    for i in range(2):
        part = jnp.where(upper, diag_in[i], 0.0)
        sym[2 * core + i] = part + part.T

    pl.semaphore_wait(barrier, len(greet))

    def to_partner(index, source, target):
        copy = pltpu.make_async_remote_copy(
            src_ref=source, dst_ref=target, send_sem=pair_send.at[index], recv_sem=pair_recv.at[index],
            device_id=partner, device_id_type=MESH,
        )
        copy.start()
        return copy

    pair = [
        to_partner(0, right_ref.at[:, pl.ds(HALF * other, HALF)], rhs.at[own]),
        to_partner(1, dst.at[own], dst.at[own]),
        to_partner(2, table_v, table_w),
        to_partner(3, blocks_ref, blocks.at[own]),
        to_partner(4, sym.at[own], sym.at[own]),
    ]

    def widen(h):
        for k in range(K):
            block = blocks[h, k]
            high = block.astype(BF16)
            w_off[h, 0:BS, k * BS : (k + 1) * BS] = high
            w_off[h, BS : 2 * BS, k * BS : (k + 1) * BS] = (block - high.astype(F32)).astype(BF16)

    def widen_sym(h):
        high = sym[h].astype(BF16)
        w_sym[h, 0:BS, :] = high
        w_sym[h, BS : 2 * BS, :] = (sym[h] - high.astype(F32)).astype(BF16)

    loads[1].wait()
    pair[0].wait_recv()
    pair[1].wait_recv()
    inverse = [1.0 / dst[h] for h in range(4)]
    u = [[rhs[h] * inverse[h] for h in range(4)]]
    image = []

    def exchange(index, j, source, target, device):
        return pltpu.make_async_remote_copy(
            src_ref=source, dst_ref=target, send_sem=ex_send.at[j, index], recv_sem=ex_recv.at[j, index],
            device_id=device, device_id_type=MESH,
        )

    def await_bytes(sem, buffer):
        pltpu.make_async_copy(buffer, buffer, sem).wait()

    def send_field(j):
        @pl.when(dom > 0)
        def _():
            for dy in (2, 1, 3, 0):
                exchange(0, j, mine.at[j], win[j].at[pl.ds(GROUP + 4 * yy, 4)], dom_at(-1, dy)).start()

        for y_here in range(1, Y):
            @pl.when(yy == y_here)
            def _():
                for y_there in range(y_here):
                    exchange(
                        1, j, mine.at[j], win[j].at[pl.ds(4 * y_here, 4)], (dom, 2 * y_there + core)
                    ).start()

    def send_products(j):
        @pl.when(dom < N_DOM - 1)
        def _():
            for dy in (2, 1, 3, 0):
                rows = pl.ds(GROUP + 4 * lax.rem(yy + dy, Y), 4)
                exchange(2, j, spread.at[j, rows], tin.at[j, Y + yy], dom_at(1, dy)).start()

        for y_here in range(Y - 1):
            @pl.when(yy == y_here)
            def _():
                for y_there in range(y_here + 1, Y):
                    exchange(
                        3, j, spread.at[j, pl.ds(4 * y_there, 4)], tin.at[j, y_here], (dom, 2 * y_there + core)
                    ).start()

    def await_field(j):
        for y_here in range(Y - 1):
            @pl.when(yy == y_here)
            def _():
                await_bytes(ex_recv.at[j, 1], win[j].at[pl.ds(0, 4 * (Y - 1 - y_here))])

        @pl.when(dom < N_DOM - 1)
        def _():
            await_bytes(ex_recv.at[j, 0], win[j].at[pl.ds(GROUP, GROUP)])

    def await_products(j):
        for y_here in range(1, Y):
            @pl.when(yy == y_here)
            def _():
                await_bytes(ex_recv.at[j, 3], win[j].at[pl.ds(0, 4 * y_here)])

        @pl.when(dom > 0)
        def _():
            await_bytes(ex_recv.at[j, 2], win[j].at[pl.ds(GROUP, GROUP)])

    def await_sends(j):
        @pl.when(dom > 0)
        def _():
            await_bytes(ex_send.at[j, 0], win[j].at[pl.ds(GROUP, GROUP)])

        @pl.when(dom < N_DOM - 1)
        def _():
            await_bytes(ex_send.at[j, 2], win[j].at[pl.ds(GROUP, GROUP)])

        for y_here in range(Y):
            @pl.when(yy == y_here)
            def _():
                if y_here:
                    await_bytes(ex_send.at[j, 1], win[j].at[pl.ds(0, 4 * y_here)])
                if y_here < Y - 1:
                    await_bytes(ex_send.at[j, 3], win[j].at[pl.ds(0, 4 * (Y - 1 - y_here))])

    def fold(out):
        return (out[0:HALF, 0:BS] + out[0:HALF, BS:]) + (out[HALF:, 0:BS] + out[HALF:, BS:])

    across = (((1,), (1,)), ((), ()))
    terms = []
    terms.append(sum(rhs[h] * u[0][h] for h in range(4)))

    for j in range(ITERS):
        field = u[j]
        for h in range(4):
            mine[j, h] = field[h]
            win[j][4 * yy + h] = field[h]
        send_field(j)
        parts = [split(field[h]) for h in range(4)]
        if j == 0:
            loads[3].wait()
            pair[2].wait_recv()
            rows = table_w[...]
            tabulate(2 * other, [rows[i, k] for i in range(2) for k in range(K)])
            pair[3].wait_recv()
            for h in range(4):
                widen(h)
        for h in range(4):
            out = jnp.dot(
                jnp.concatenate([parts[h], parts[h]], axis=1), w_off[h], preferred_element_type=F32
            )
            for k in range(K):
                prods[5 * h + k] = out[0:HALF, k * BS : (k + 1) * BS] + out[HALF:, k * BS : (k + 1) * BS]
        for w in range(2 * GROUP):
            picked = [prods[slot_s[h * 2 * GROUP + w]] for h in range(4)]
            spread[j, w] = (picked[0] + picked[1]) + (picked[2] + picked[3])
        send_products(j)
        if j == 0:
            pair[4].wait_recv()
            for h in range(4):
                widen_sym(h)
        near = [
            fold(lax.dot_general(parts[h], w_sym[h], across, preferred_element_type=F32)) for h in range(4)
        ]
        await_field(j)
        ahead = []
        for h in range(4):
            tiles = [split(win[j][place_s[h * K + k]]) for k in range(K)]
            ahead.append(
                fold(
                    lax.dot_general(
                        jnp.concatenate(tiles, axis=1), w_off[h], across, preferred_element_type=F32
                    )
                )
            )
        if j == ITERS - 1:
            terms.append(sum(field[h] * (2.0 * ahead[h] + near[h]) for h in range(4)))
        else:
            await_products(j)
            applied = []
            for h in range(4):
                back = spread[j, 4 * yy + h]
                for s in range(2 * Y):
                    back = back + tin[j, s, h]
                applied.append(near[h] + ahead[h] + back)
            image.append(applied)
            u.append([applied[h] * inverse[h] for h in range(4)])
            terms.append(sum(field[h] * applied[h] for h in range(4)))
            terms.append(sum(u[j + 1][h] * applied[h] for h in range(4)))

    lanes = lax.broadcasted_iota(I32, (HALF, BS), 1)
    tile = jnp.zeros((HALF, BS), F32)
    for index, term in enumerate(terms):
        tile = jnp.where(lanes == index, jnp.sum(term, axis=1, keepdims=True), tile)

    def reduced(stage, buffer, slot, devices, tile):
        red_src[stage] = tile
        buffer[slot] = tile
        for device in devices:
            pltpu.make_async_remote_copy(
                src_ref=red_src.at[stage], dst_ref=buffer.at[slot], send_sem=red_send.at[stage],
                recv_sem=red_recv.at[stage], device_id=device, device_id_type=MESH,
            ).start()

    def total(stage, buffer, count):
        await_bytes(red_recv.at[stage], buffer.at[pl.ds(0, count - 1)])
        values = [buffer[i] for i in range(count)]
        while len(values) > 1:
            values = [values[i] + values[i + 1] for i in range(0, len(values), 2)]
        return values[0]

    reduced(0, red_a, Y * xx + yy, [at(dx, dy, 0) for dx, dy in plane], tile)
    last = ITERS - 1
    await_products(last)
    applied = []
    for h in range(4):
        back = spread[last, 4 * yy + h]
        for s in range(2 * Y):
            back = back + tin[last, s, h]
        applied.append(near[h] + ahead[h] + back)
    image.append(applied)
    tile = total(0, red_a, X * Y)
    reduced(1, red_b, zz, [at(0, 0, dz) for dz in ring_order(Z)], tile)
    tile = total(1, red_b, Z)

    gram = [jnp.broadcast_to(tile[:, i : i + 1], (HALF, BS)) for i in range(2 * ITERS)]

    def inner(a, b):
        value = None
        for i in range(len(a)):
            for k in range(len(b)):
                if a[i] is not None and b[k] is not None:
                    term = a[i] * b[k] * gram[i + k]
                    value = term if value is None else value + term
        return value

    def plus(a, b):
        return a if b is None else b if a is None else a + b

    one = jnp.ones((HALF, BS), F32)
    zc, pc, xc = [one, None, None, None], [one, None, None], [None, None, None]
    rho = gram[0]
    for step in range(ITERS):
        ac = [pc[0], plus(pc[1], pc[0]), plus(pc[2], pc[1]), pc[2]]
        alpha = rho / inner(pc, ac)
        xc = [plus(xc[i], None if pc[i] is None else alpha * pc[i]) for i in range(3)]
        zc = [plus(zc[i], None if ac[i] is None else -alpha * ac[i]) for i in range(4)]
        if step < ITERS - 1:
            fresh = inner(zc, zc)
            beta = fresh / rho
            pc = [plus(zc[i], None if pc[i] is None else beta * pc[i]) for i in range(3)]
            rho = fresh

    for h in range(4):
        outs[0, h] = xc[0] * u[0][h] + xc[1] * u[1][h] + xc[2] * u[2][h]
        outs[1, h] = zc[0] * rhs[h] + zc[1] * image[0][h] + zc[2] * image[1][h] + zc[3] * image[2][h]

    mine_half = pl.ds(HALF * core, HALF)
    ends = []
    for i, out in enumerate((x_out, res_out)):
        ends.append(to_partner(5 + i, outs.at[i, theirs], out.at[:, mine_half]))
        keep = pltpu.make_async_copy(outs.at[i, own], out.at[:, mine_half], local_sems.at[5 + i])
        keep.start()
        ends.append(keep)
    for j in range(ITERS):
        await_sends(j)
    await_bytes(red_send.at[0], red_a.at[pl.ds(0, X * Y - 1)])
    await_bytes(red_send.at[1], red_b.at[pl.ds(0, Z - 1)])
    for copy in pair:
        copy.wait_send()
    for copy in ends:
        copy.wait()


def local(right_side, diag_blocks, block_values, block_cols, block_count, cell_diagonal):
    hbm = pl.BlockSpec(memory_space=pl.ANY)
    smem = pl.BlockSpec(memory_space=pltpu.SMEM)
    shape = jax.ShapeDtypeStruct(right_side.shape, F32)
    return pl.pallas_call(
        kernel,
        out_shape=(shape, shape),
        in_specs=[hbm, hbm, hbm, smem, smem, hbm],
        out_specs=(hbm, hbm),
        scratch_shapes=[
            pltpu.VMEM((4, HALF, BS), F32),
            pltpu.VMEM((4, HALF, BS), F32),
            pltpu.VMEM((2, BS, BS), F32),
            pltpu.VMEM((2, BS), F32),
            pltpu.VMEM((4, BS, BS), F32),
            pltpu.VMEM((4, K, BS, BS), F32),
            pltpu.VMEM((8, BS), I32),
            pltpu.VMEM((8, BS), I32),
            pltpu.SMEM((4 * K,), I32),
            pltpu.SMEM((4 * 2 * GROUP,), I32),
            pltpu.VMEM((4, 2 * BS, K * BS), BF16),
            pltpu.VMEM((4, 2 * BS, BS), BF16),
            pltpu.VMEM((ITERS, 4, HALF, BS), F32),
            pltpu.VMEM((2 * GROUP + 1, HALF, BS), F32),
            pltpu.VMEM((2 * GROUP + 1, HALF, BS), F32),
            pltpu.VMEM((2 * GROUP + 1, HALF, BS), F32),
            pltpu.VMEM((4 * (K + 1), HALF, BS), F32),
            pltpu.VMEM((ITERS, 2 * GROUP, HALF, BS), F32),
            pltpu.VMEM((ITERS, 2 * Y, 4, HALF, BS), F32),
            pltpu.VMEM((2, HALF, BS), F32),
            pltpu.VMEM((X * Y, HALF, BS), F32),
            pltpu.VMEM((Z, HALF, BS), F32),
            pltpu.VMEM((2, 4, HALF, BS), F32),
            pltpu.SemaphoreType.DMA((7,)),
            pltpu.SemaphoreType.DMA((7,)),
            pltpu.SemaphoreType.DMA((7,)),
            pltpu.SemaphoreType.DMA((ITERS, 4)),
            pltpu.SemaphoreType.DMA((ITERS, 4)),
            pltpu.SemaphoreType.DMA((2,)),
            pltpu.SemaphoreType.DMA((2,)),
        ],
        compiler_params=pltpu.CompilerParams(
            collective_id=0, has_side_effects=True, vmem_limit_bytes=24 << 20
        ),
        name="cg",
    )(right_side, diag_blocks, block_values, block_cols, block_count, cell_diagonal)


def solution(mesh):
    rows = P(("dom", "sub"))
    return jax.shard_map(
        local,
        mesh=mesh,
        in_specs=(rows,) * 6,
        out_specs=(rows, rows),
        check_vma=False,
    )
```

```python
import functools

import jax
import jax.numpy as jnp
from jax import lax
from jax.experimental import pallas as pl
from jax.experimental.pallas import tpu as pltpu
from jax.sharding import PartitionSpec as P

MESH = pl.DeviceIdType.MESH
K = 4
ITERS = 3
BS = 128
HALF = 8
X, Y, Z = 4, 4, 16
N_DOM = X * Z
GROUP = 4 * Y
F32, BF16, I32 = jnp.float32, jnp.bfloat16, jnp.int32


def ring_order(n):
    return sorted(range(1, n), key=lambda d: -min(d, n - d))


def split(v):
    high = v.astype(BF16).astype(F32)
    return jnp.concatenate([high, v - high], axis=0).astype(BF16)


def kernel(
    right_ref, diag_ref, blocks_ref, cols_ref, celld_ref, out_ref,
    rhs, dst, diag_in, dcell, sym, blocks, cols_v, place_s, slot_s, w_off, w_sym,
    mine, win_0, win_1, win_2, prods, spread, tin, red_src, red_a, red_b, outs,
    local_sems, pair_send, pair_recv, ex_send, ex_recv, red_send, red_recv, meet,
):
    dom, sub = lax.axis_index("dom"), lax.axis_index("sub")
    xx, zz = dom // Z, lax.rem(dom, Z)
    yy, core = sub // 2, lax.rem(sub, 2)
    other = 1 - core
    own = pl.ds(2 * core, 2)
    theirs = pl.ds(2 * other, 2)
    partner = (dom, 2 * yy + other)

    def at(dx, dy, dz):
        return (
            lax.rem(xx + dx, X) * Z + lax.rem(zz + dz, Z),
            2 * lax.rem(yy + dy, Y) + core,
        )

    def dom_at(step, dy):
        return (lax.rem(dom + step + N_DOM, N_DOM), 2 * lax.rem(yy + dy, Y) + core)

    loads = [
        pltpu.make_async_copy(celld_ref, dcell, local_sems.at[0]),
        pltpu.make_async_copy(right_ref.at[:, pl.ds(HALF * core, HALF)], rhs.at[own], local_sems.at[1]),
        pltpu.make_async_copy(diag_ref, diag_in, local_sems.at[2]),
        pltpu.make_async_copy(blocks_ref, blocks.at[own], local_sems.at[3]),
        pltpu.make_async_copy(cols_ref, cols_v.at[core], local_sems.at[4]),
    ]
    for load in loads:
        load.start()

    win = (win_0, win_1, win_2)
    for window in win:
        window[...] = jnp.zeros_like(window)
    tin[...] = jnp.zeros_like(tin)

    barrier = pltpu.get_barrier_semaphore()
    plane = [(dx, dy) for dx in range(X) for dy in range(Y) if dx or dy]
    plane.sort(key=lambda p: -(min(p[0], X - p[0]) + min(p[1], Y - p[1])))
    greet = [dom_at(step, dy) for dy in (2, 1, 3, 0) for step in (1, -1)]
    greet += [at(0, 0, dz) for dz in (1, Z - 1)]
    greet += [at(dx, dy, 0) for dx, dy in plane]

    @pl.when(core == 0)
    def _():
        pl.semaphore_signal(barrier, inc=1, device_id=partner, device_id_type=MESH)

    for to_dom, to_sub in greet:
        pl.semaphore_signal(
            barrier, inc=1, device_id=(to_dom, to_sub - core), device_id_type=MESH
        )

    def to_partner(index, source, target):
        copy = pltpu.make_async_remote_copy(
            src_ref=source, dst_ref=target, send_sem=pair_send.at[index], recv_sem=pair_recv.at[index],
            device_id=partner, device_id_type=MESH,
        )
        copy.start()
        return copy

    @pl.when(core == 1)
    def _():
        pl.semaphore_wait(barrier, 1)
        pl.semaphore_signal(meet.at[0], inc=1, device_id=partner, device_id_type=MESH)

    @pl.when(core == 0)
    def _():
        pl.semaphore_wait(meet.at[0], 1)

    pair = [
        to_partner(0, right_ref.at[:, pl.ds(HALF * other, HALF)], rhs.at[own]),
        to_partner(2, cols_ref, cols_v.at[core]),
        to_partner(3, blocks_ref, blocks.at[own]),
    ]

    for h in range(4):
        prods[5 * h + K] = jnp.zeros((HALF, BS), F32)
    def tabulate(which):
        base = 2 * which
        columns = cols_v[which]
        places = [columns[i, k] for i in range(2) for k in range(K)]
        places = [jnp.where(place > 0, place, 2 * GROUP) for place in places]
        for i in range(2):
            for k in range(K):
                place_s[(base + i) * K + k] = places[i * K + k]
            for w in range(2 * GROUP):
                slot = K
                for k in range(K):
                    slot = jnp.where(places[i * K + k] == w, k, slot)
                slot_s[(base + i) * 2 * GROUP + w] = slot + (base + i) * (K + 1)

    loads[4].wait()
    tabulate(core)

    loads[0].wait()
    for i in range(2):
        dst[2 * core + i] = jnp.broadcast_to(dcell[i : i + 1, :], (HALF, BS))
    pair.insert(1, to_partner(1, dst.at[own], dst.at[own]))
    loads[2].wait()
    upper = lax.broadcasted_iota(I32, (BS, BS), 0) < lax.broadcasted_iota(I32, (BS, BS), 1)
    for i in range(2):
        part = jnp.where(upper, diag_in[i], 0.0)
        sym[2 * core + i] = part + part.T
    pair.append(to_partner(4, sym.at[own], sym.at[own]))

    @pl.when(core == 0)
    def _():
        pl.semaphore_wait(barrier, 2 * len(greet))
        pl.semaphore_signal(meet.at[0], inc=1, device_id=partner, device_id_type=MESH)

    @pl.when(core == 1)
    def _():
        pl.semaphore_wait(meet.at[0], 1)

    def hail(step, distance):
        for dz in (distance, Z - distance):
            pl.semaphore_signal(meet.at[step], inc=1, device_id=at(0, 0, dz), device_id_type=MESH)

    hail(1, 1)

    def widen(h):
        for k in range(K):
            block = blocks[h, k]
            high = block.astype(BF16)
            w_off[h, 0:BS, k * BS : (k + 1) * BS] = high
            w_off[h, BS : 2 * BS, k * BS : (k + 1) * BS] = (block - high.astype(F32)).astype(BF16)

    def widen_sym(h):
        high = sym[h].astype(BF16)
        w_sym[h, 0:BS, :] = high
        w_sym[h, BS : 2 * BS, :] = (sym[h] - high.astype(F32)).astype(BF16)

    loads[1].wait()
    pair[0].wait_recv()
    pair[1].wait_recv()
    inverse = [1.0 / dst[h] for h in range(4)]
    u = [[rhs[h] * inverse[h] for h in range(4)]]
    image = []

    def exchange(index, j, source, target, device):
        return pltpu.make_async_remote_copy(
            src_ref=source, dst_ref=target, send_sem=ex_send.at[j, index], recv_sem=ex_recv.at[j, index],
            device_id=device, device_id_type=MESH,
        )

    def await_bytes(sem, buffer):
        pltpu.make_async_copy(buffer, buffer, sem).wait()

    def send_field(j):
        @pl.when(dom > 0)
        def _():
            for dy in (2, 1, 3, 0):
                exchange(0, j, mine.at[j], win[j].at[pl.ds(GROUP + 4 * yy, 4)], dom_at(-1, dy)).start()

        for y_here in range(1, Y):
            @pl.when(yy == y_here)
            def _():
                for y_there in range(y_here):
                    exchange(
                        1, j, mine.at[j], win[j].at[pl.ds(4 * y_here, 4)], (dom, 2 * y_there + core)
                    ).start()

    def send_products(j):
        @pl.when(dom < N_DOM - 1)
        def _():
            for dy in (2, 1, 3, 0):
                rows = pl.ds(GROUP + 4 * lax.rem(yy + dy, Y), 4)
                exchange(2, j, spread.at[j, rows], tin.at[j, Y + yy], dom_at(1, dy)).start()

        for y_here in range(Y - 1):
            @pl.when(yy == y_here)
            def _():
                for y_there in range(y_here + 1, Y):
                    exchange(
                        3, j, spread.at[j, pl.ds(4 * y_there, 4)], tin.at[j, y_here], (dom, 2 * y_there + core)
                    ).start()

    def await_field(j):
        for y_here in range(Y - 1):
            @pl.when(yy == y_here)
            def _():
                await_bytes(ex_recv.at[j, 1], win[j].at[pl.ds(0, 4 * (Y - 1 - y_here))])

        @pl.when(dom < N_DOM - 1)
        def _():
            await_bytes(ex_recv.at[j, 0], win[j].at[pl.ds(GROUP, GROUP)])

    def await_products(j):
        for y_here in range(1, Y):
            @pl.when(yy == y_here)
            def _():
                await_bytes(ex_recv.at[j, 3], win[j].at[pl.ds(0, 4 * y_here)])

        @pl.when(dom > 0)
        def _():
            await_bytes(ex_recv.at[j, 2], win[j].at[pl.ds(GROUP, GROUP)])

    def await_sends(j):
        @pl.when(dom > 0)
        def _():
            await_bytes(ex_send.at[j, 0], win[j].at[pl.ds(GROUP, GROUP)])

        @pl.when(dom < N_DOM - 1)
        def _():
            await_bytes(ex_send.at[j, 2], win[j].at[pl.ds(GROUP, GROUP)])

        for y_here in range(Y):
            @pl.when(yy == y_here)
            def _():
                if y_here:
                    await_bytes(ex_send.at[j, 1], win[j].at[pl.ds(0, 4 * y_here)])
                if y_here < Y - 1:
                    await_bytes(ex_send.at[j, 3], win[j].at[pl.ds(0, 4 * (Y - 1 - y_here))])

    def fold(out):
        return (out[0:HALF, 0:BS] + out[0:HALF, BS:]) + (out[HALF:, 0:BS] + out[HALF:, BS:])

    across = (((1,), (1,)), ((), ()))
    terms = []
    terms.append(sum(rhs[h] * u[0][h] for h in range(4)))

    for j in range(ITERS):
        field = u[j]
        for h in range(4):
            mine[j, h] = field[h]
            win[j][4 * yy + h] = field[h]
        send_field(j)
        parts = [split(field[h]) for h in range(4)]
        if j == 0:
            loads[3].wait()
            pair[2].wait_recv()
            tabulate(other)
            pair[3].wait_recv()
            for h in range(4):
                widen(h)
        for h in range(4):
            out = jnp.dot(
                jnp.concatenate([parts[h], parts[h]], axis=1), w_off[h], preferred_element_type=F32
            )
            for k in range(K):
                prods[5 * h + k] = out[0:HALF, k * BS : (k + 1) * BS] + out[HALF:, k * BS : (k + 1) * BS]
        for w in range(2 * GROUP):
            picked = [prods[slot_s[h * 2 * GROUP + w]] for h in range(4)]
            spread[j, w] = (picked[0] + picked[1]) + (picked[2] + picked[3])
        send_products(j)
        if j == 0:
            pair[4].wait_recv()
            for h in range(4):
                widen_sym(h)
        near = [
            fold(lax.dot_general(parts[h], w_sym[h], across, preferred_element_type=F32)) for h in range(4)
        ]
        await_field(j)
        ahead = []
        for h in range(4):
            tiles = [split(win[j][place_s[h * K + k]]) for k in range(K)]
            ahead.append(
                fold(
                    lax.dot_general(
                        jnp.concatenate(tiles, axis=1), w_off[h], across, preferred_element_type=F32
                    )
                )
            )
        pl.semaphore_wait(meet.at[j + 1], 2)
        if j < ITERS - 1:
            hail(j + 2, 2 << j)
        if j == ITERS - 1:
            terms.append(sum(field[h] * (2.0 * ahead[h] + near[h]) for h in range(4)))
        else:
            await_products(j)
            applied = []
            for h in range(4):
                back = spread[j, 4 * yy + h]
                for s in range(2 * Y):
                    back = back + tin[j, s, h]
                applied.append(near[h] + ahead[h] + back)
            image.append(applied)
            u.append([applied[h] * inverse[h] for h in range(4)])
            terms.append(sum(field[h] * applied[h] for h in range(4)))
            terms.append(sum(u[j + 1][h] * applied[h] for h in range(4)))

    lanes = lax.broadcasted_iota(I32, (HALF, BS), 1)
    tile = jnp.zeros((HALF, BS), F32)
    for index, term in enumerate(terms):
        tile = jnp.where(lanes == index, jnp.sum(term, axis=1, keepdims=True), tile)

    def reduced(stage, buffer, slot, devices, tile):
        red_src[stage] = tile
        buffer[slot] = tile
        for device in devices:
            pltpu.make_async_remote_copy(
                src_ref=red_src.at[stage], dst_ref=buffer.at[slot], send_sem=red_send.at[stage],
                recv_sem=red_recv.at[stage], device_id=device, device_id_type=MESH,
            ).start()

    def total(stage, buffer, count):
        await_bytes(red_recv.at[stage], buffer.at[pl.ds(0, count - 1)])
        values = [buffer[i] for i in range(count)]
        while len(values) > 1:
            values = [values[i] + values[i + 1] for i in range(0, len(values), 2)]
        return values[0]

    reduced(0, red_a, Y * xx + yy, [at(dx, dy, 0) for dx, dy in plane], tile)
    last = ITERS - 1
    await_products(last)
    applied = []
    for h in range(4):
        back = spread[last, 4 * yy + h]
        for s in range(2 * Y):
            back = back + tin[last, s, h]
        applied.append(near[h] + ahead[h] + back)
    image.append(applied)
    tile = total(0, red_a, X * Y)
    reduced(1, red_b, zz, [at(0, 0, dz) for dz in ring_order(Z)], tile)
    tile = total(1, red_b, Z)

    gram = [jnp.broadcast_to(tile[:, i : i + 1], (HALF, BS)) for i in range(2 * ITERS)]

    def inner(a, b):
        value = None
        for i in range(len(a)):
            for k in range(len(b)):
                if a[i] is not None and b[k] is not None:
                    term = a[i] * b[k] * gram[i + k]
                    value = term if value is None else value + term
        return value

    def plus(a, b):
        return a if b is None else b if a is None else a + b

    one = jnp.ones((HALF, BS), F32)
    zc, pc, xc = [one, None, None, None], [one, None, None], [None, None, None]
    rho = gram[0]
    for step in range(ITERS):
        ac = [pc[0], plus(pc[1], pc[0]), plus(pc[2], pc[1]), pc[2]]
        alpha = rho / inner(pc, ac)
        xc = [plus(xc[i], None if pc[i] is None else alpha * pc[i]) for i in range(3)]
        zc = [plus(zc[i], None if ac[i] is None else -alpha * ac[i]) for i in range(4)]
        if step < ITERS - 1:
            fresh = inner(zc, zc)
            beta = fresh / rho
            pc = [plus(zc[i], None if pc[i] is None else beta * pc[i]) for i in range(3)]
            rho = fresh

    for h in range(4):
        outs[0, h] = xc[0] * u[0][h] + xc[1] * u[1][h] + xc[2] * u[2][h]
        outs[1, h] = zc[0] * rhs[h] + zc[1] * image[0][h] + zc[2] * image[1][h] + zc[3] * image[2][h]

    mine_half = pl.ds(HALF * core, HALF)
    ends = []
    for i in range(2):
        ends.append(to_partner(5 + i, outs.at[i, theirs], out_ref.at[i, :, mine_half]))
        keep = pltpu.make_async_copy(outs.at[i, own], out_ref.at[i, :, mine_half], local_sems.at[5 + i])
        keep.start()
        ends.append(keep)
    for j in range(ITERS):
        await_sends(j)
    await_bytes(red_send.at[0], red_a.at[pl.ds(0, X * Y - 1)])
    await_bytes(red_send.at[1], red_b.at[pl.ds(0, Z - 1)])
    for copy in pair:
        copy.wait_send()
    for copy in ends:
        copy.wait()


def local(right_side, diag_blocks, block_values, block_cols, block_count, cell_diagonal):
    hbm = pl.BlockSpec(memory_space=pl.ANY)
    both = pl.pallas_call(
        kernel,
        out_shape=jax.ShapeDtypeStruct((2, *right_side.shape), F32),
        in_specs=[hbm] * 5,
        out_specs=hbm,
        scratch_shapes=[
            pltpu.VMEM((4, HALF, BS), F32),
            pltpu.VMEM((4, HALF, BS), F32),
            pltpu.VMEM((2, BS, BS), F32),
            pltpu.VMEM((2, BS), F32),
            pltpu.VMEM((4, BS, BS), F32),
            pltpu.VMEM((4, K, BS, BS), F32),
            pltpu.VMEM((2, 2, K), I32),
            pltpu.SMEM((4 * K,), I32),
            pltpu.SMEM((4 * 2 * GROUP,), I32),
            pltpu.VMEM((4, 2 * BS, K * BS), BF16),
            pltpu.VMEM((4, 2 * BS, BS), BF16),
            pltpu.VMEM((ITERS, 4, HALF, BS), F32),
            pltpu.VMEM((2 * GROUP + 1, HALF, BS), F32),
            pltpu.VMEM((2 * GROUP + 1, HALF, BS), F32),
            pltpu.VMEM((2 * GROUP + 1, HALF, BS), F32),
            pltpu.VMEM((4 * (K + 1), HALF, BS), F32),
            pltpu.VMEM((ITERS, 2 * GROUP, HALF, BS), F32),
            pltpu.VMEM((ITERS, 2 * Y, 4, HALF, BS), F32),
            pltpu.VMEM((2, HALF, BS), F32),
            pltpu.VMEM((X * Y, HALF, BS), F32),
            pltpu.VMEM((Z, HALF, BS), F32),
            pltpu.VMEM((2, 4, HALF, BS), F32),
            pltpu.SemaphoreType.DMA((7,)),
            pltpu.SemaphoreType.DMA((7,)),
            pltpu.SemaphoreType.DMA((7,)),
            pltpu.SemaphoreType.DMA((ITERS, 4)),
            pltpu.SemaphoreType.DMA((ITERS, 4)),
            pltpu.SemaphoreType.DMA((2,)),
            pltpu.SemaphoreType.DMA((2,)),
            pltpu.SemaphoreType.REGULAR((4,)),
        ],
        compiler_params=pltpu.CompilerParams(
            collective_id=0, has_side_effects=True, vmem_limit_bytes=60 << 20
        ),
        name="cg",
    )(right_side, diag_blocks, block_values, block_cols, cell_diagonal)
    return both[0], both[1]


def solution(mesh):
    rows = P(("dom", "sub"))
    return jax.shard_map(
        local,
        mesh=mesh,
        in_specs=(rows,) * 6,
        out_specs=(rows, rows),
        check_vma=False,
    )
```

```python
import functools

import jax
import jax.numpy as jnp
from jax import lax
from jax.experimental import pallas as pl
from jax.experimental.pallas import tpu as pltpu
from jax.sharding import PartitionSpec as P

MESH = pl.DeviceIdType.MESH
K = 4
ITERS = 3
BS = 128
HALF = 8
X, Y, Z = 4, 4, 16
N_DOM = X * Z
GROUP = 4 * Y
F32, BF16, I32 = jnp.float32, jnp.bfloat16, jnp.int32


def ring_order(n):
    return sorted(range(1, n), key=lambda d: -min(d, n - d))


def split(v):
    high = v.astype(BF16).astype(F32)
    return jnp.concatenate([high, v - high], axis=0).astype(BF16)


def kernel(
    right_ref, diag_ref, blocks_ref, cols_ref, celld_ref, out_ref,
    rhs, dst, diag_in, dcell, sym, blocks, cols_v, place_s, slot_s, w_off, w_sym,
    mine, win_0, win_1, win_2, prods, spread, tin, red_src, red_a, red_b, outs,
    local_sems, pair_send, pair_recv, ex_send, ex_recv, red_send, red_recv, meet,
):
    dom, sub = lax.axis_index("dom"), lax.axis_index("sub")
    xx, zz = dom // Z, lax.rem(dom, Z)
    yy, core = sub // 2, lax.rem(sub, 2)
    other = 1 - core
    own = pl.ds(2 * core, 2)
    theirs = pl.ds(2 * other, 2)
    partner = (dom, 2 * yy + other)

    def at(dx, dy, dz):
        return (
            lax.rem(xx + dx, X) * Z + lax.rem(zz + dz, Z),
            2 * lax.rem(yy + dy, Y) + core,
        )

    def dom_at(step, dy):
        return (lax.rem(dom + step + N_DOM, N_DOM), 2 * lax.rem(yy + dy, Y) + core)

    loads = [
        pltpu.make_async_copy(celld_ref, dcell, local_sems.at[0]),
        pltpu.make_async_copy(right_ref.at[:, pl.ds(HALF * core, HALF)], rhs.at[own], local_sems.at[1]),
        pltpu.make_async_copy(diag_ref, diag_in, local_sems.at[2]),
        pltpu.make_async_copy(blocks_ref, blocks.at[own], local_sems.at[3]),
        pltpu.make_async_copy(cols_ref, cols_v.at[core], local_sems.at[4]),
    ]
    for load in loads:
        load.start()

    win = (win_0, win_1, win_2)
    for window in win:
        window[...] = jnp.zeros_like(window)
    tin[...] = jnp.zeros_like(tin)

    barrier = pltpu.get_barrier_semaphore()
    plane = [(dx, dy) for dx in range(X) for dy in range(Y) if dx or dy]
    plane.sort(key=lambda p: -(min(p[0], X - p[0]) + min(p[1], Y - p[1])))
    greet = [dom_at(step, dy) for dy in (2, 1, 3, 0) for step in (1, -1)]
    greet += [at(0, 0, dz) for dz in (1, 2, Z - 2, Z - 1)]
    greet += [at(dx, dy, 0) for dx, dy in plane]

    @pl.when(core == 0)
    def _():
        pl.semaphore_signal(barrier, inc=1, device_id=partner, device_id_type=MESH)

    for to_dom, to_sub in greet:
        pl.semaphore_signal(
            barrier, inc=1, device_id=(to_dom, to_sub - core), device_id_type=MESH
        )

    def to_partner(index, source, target):
        copy = pltpu.make_async_remote_copy(
            src_ref=source, dst_ref=target, send_sem=pair_send.at[index], recv_sem=pair_recv.at[index],
            device_id=partner, device_id_type=MESH,
        )
        copy.start()
        return copy

    @pl.when(core == 1)
    def _():
        pl.semaphore_wait(barrier, 1)
        pl.semaphore_signal(meet.at[0], inc=1, device_id=partner, device_id_type=MESH)

    @pl.when(core == 0)
    def _():
        pl.semaphore_wait(meet.at[0], 1)

    pair = [
        to_partner(0, right_ref.at[:, pl.ds(HALF * other, HALF)], rhs.at[own]),
        to_partner(2, cols_ref, cols_v.at[core]),
        to_partner(3, blocks_ref, blocks.at[own]),
    ]

    for h in range(4):
        prods[5 * h + K] = jnp.zeros((HALF, BS), F32)
    def tabulate(which):
        base = 2 * which
        columns = cols_v[which]
        places = [columns[i, k] for i in range(2) for k in range(K)]
        places = [jnp.where(place > 0, place, 2 * GROUP) for place in places]
        for i in range(2):
            for k in range(K):
                place_s[(base + i) * K + k] = places[i * K + k]
            for w in range(2 * GROUP):
                slot = K
                for k in range(K):
                    slot = jnp.where(places[i * K + k] == w, k, slot)
                slot_s[(base + i) * 2 * GROUP + w] = slot + (base + i) * (K + 1)

    loads[4].wait()
    tabulate(core)

    loads[0].wait()
    for i in range(2):
        dst[2 * core + i] = jnp.broadcast_to(dcell[i : i + 1, :], (HALF, BS))
    pair.insert(1, to_partner(1, dst.at[own], dst.at[own]))
    loads[2].wait()
    upper = lax.broadcasted_iota(I32, (BS, BS), 0) < lax.broadcasted_iota(I32, (BS, BS), 1)
    for i in range(2):
        part = jnp.where(upper, diag_in[i], 0.0)
        sym[2 * core + i] = part + part.T
    pair.append(to_partner(4, sym.at[own], sym.at[own]))

    @pl.when(core == 0)
    def _():
        pl.semaphore_wait(barrier, 2 * len(greet))
        pl.semaphore_signal(meet.at[0], inc=1, device_id=partner, device_id_type=MESH)

    @pl.when(core == 1)
    def _():
        pl.semaphore_wait(meet.at[0], 1)

    reach = ((1, 2, Z - 2, Z - 1), (4, Z - 4), (6, Z - 6))

    def hail(step):
        for dz in reach[step]:
            pl.semaphore_signal(meet.at[step + 1], inc=1, device_id=at(0, 0, dz), device_id_type=MESH)

    hail(0)

    def widen(h):
        for k in range(K):
            block = blocks[h, k]
            high = block.astype(BF16)
            w_off[h, 0:BS, k * BS : (k + 1) * BS] = high
            w_off[h, BS : 2 * BS, k * BS : (k + 1) * BS] = (block - high.astype(F32)).astype(BF16)

    def widen_sym(h):
        high = sym[h].astype(BF16)
        w_sym[h, 0:BS, :] = high
        w_sym[h, BS : 2 * BS, :] = (sym[h] - high.astype(F32)).astype(BF16)

    loads[1].wait()
    pair[0].wait_recv()
    pair[1].wait_recv()
    inverse = [1.0 / dst[h] for h in range(4)]
    u = [[rhs[h] * inverse[h] for h in range(4)]]
    image = []

    def exchange(index, j, source, target, device):
        return pltpu.make_async_remote_copy(
            src_ref=source, dst_ref=target, send_sem=ex_send.at[j, index], recv_sem=ex_recv.at[j, index],
            device_id=device, device_id_type=MESH,
        )

    def await_bytes(sem, buffer):
        pltpu.make_async_copy(buffer, buffer, sem).wait()

    def send_field_back(j, order):
        @pl.when(dom > 0)
        def _():
            for dy in order:
                exchange(0, j, mine.at[j], win[j].at[pl.ds(GROUP + 4 * yy, 4)], dom_at(-1, dy)).start()

    def send_field_own(j):
        for y_here in range(1, Y):
            @pl.when(yy == y_here)
            def _():
                for y_there in range(y_here):
                    exchange(
                        1, j, mine.at[j], win[j].at[pl.ds(4 * y_here, 4)], (dom, 2 * y_there + core)
                    ).start()

    def send_products_on(j, order):
        @pl.when(dom < N_DOM - 1)
        def _():
            for dy in order:
                rows = pl.ds(GROUP + 4 * lax.rem(yy + dy, Y), 4)
                exchange(2, j, spread.at[j, rows], tin.at[j, Y + yy], dom_at(1, dy)).start()

    def send_products_own(j):
        for y_here in range(Y - 1):
            @pl.when(yy == y_here)
            def _():
                for y_there in range(y_here + 1, Y):
                    exchange(
                        3, j, spread.at[j, pl.ds(4 * y_there, 4)], tin.at[j, y_here], (dom, 2 * y_there + core)
                    ).start()

    def await_field(j):
        for y_here in range(Y - 1):
            @pl.when(yy == y_here)
            def _():
                await_bytes(ex_recv.at[j, 1], win[j].at[pl.ds(0, 4 * (Y - 1 - y_here))])

        @pl.when(dom < N_DOM - 1)
        def _():
            await_bytes(ex_recv.at[j, 0], win[j].at[pl.ds(GROUP, GROUP)])

    def await_products(j):
        for y_here in range(1, Y):
            @pl.when(yy == y_here)
            def _():
                await_bytes(ex_recv.at[j, 3], win[j].at[pl.ds(0, 4 * y_here)])

        @pl.when(dom > 0)
        def _():
            await_bytes(ex_recv.at[j, 2], win[j].at[pl.ds(GROUP, GROUP)])

    def await_sends(j):
        @pl.when(dom > 0)
        def _():
            await_bytes(ex_send.at[j, 0], win[j].at[pl.ds(GROUP, GROUP)])

        @pl.when(dom < N_DOM - 1)
        def _():
            await_bytes(ex_send.at[j, 2], win[j].at[pl.ds(GROUP, GROUP)])

        for y_here in range(Y):
            @pl.when(yy == y_here)
            def _():
                if y_here:
                    await_bytes(ex_send.at[j, 1], win[j].at[pl.ds(0, 4 * y_here)])
                if y_here < Y - 1:
                    await_bytes(ex_send.at[j, 3], win[j].at[pl.ds(0, 4 * (Y - 1 - y_here))])

    def fold(out):
        return (out[0:HALF, 0:BS] + out[0:HALF, BS:]) + (out[HALF:, 0:BS] + out[HALF:, BS:])

    across = (((1,), (1,)), ((), ()))
    terms = []
    terms.append(sum(rhs[h] * u[0][h] for h in range(4)))

    for j in range(ITERS):
        field = u[j]
        for h in range(4):
            mine[j, h] = field[h]
            win[j][4 * yy + h] = field[h]
        send_field_back(j, (2,))
        parts = [split(field[h]) for h in range(4)]
        if j == 0:
            loads[3].wait()
            pair[2].wait_recv()
            tabulate(other)
            pair[3].wait_recv()
            for h in range(4):
                widen(h)
        for h in range(4):
            out = jnp.dot(
                jnp.concatenate([parts[h], parts[h]], axis=1), w_off[h], preferred_element_type=F32
            )
            for k in range(K):
                prods[5 * h + k] = out[0:HALF, k * BS : (k + 1) * BS] + out[HALF:, k * BS : (k + 1) * BS]

        def gather_products(first):
            for w in range(first, first + GROUP):
                picked = [prods[slot_s[h * 2 * GROUP + w]] for h in range(4)]
                spread[j, w] = (picked[0] + picked[1]) + (picked[2] + picked[3])

        gather_products(GROUP)
        send_products_on(j, (2,))
        send_field_back(j, (1, 3))
        send_products_on(j, (1, 3))
        send_field_own(j)
        gather_products(0)
        send_products_own(j)
        send_field_back(j, (0,))
        send_products_on(j, (0,))
        if j == 0:
            pair[4].wait_recv()
            for h in range(4):
                widen_sym(h)
        near = [
            fold(lax.dot_general(parts[h], w_sym[h], across, preferred_element_type=F32)) for h in range(4)
        ]
        if j == ITERS - 1:
            await_field(j)
            pl.semaphore_wait(meet.at[j + 1], len(reach[j]))
        else:
            pl.semaphore_wait(meet.at[j + 1], len(reach[j]))
            hail(j + 1)
            await_field(j)
        ahead = []
        for h in range(4):
            tiles = [split(win[j][place_s[h * K + k]]) for k in range(K)]
            ahead.append(
                fold(
                    lax.dot_general(
                        jnp.concatenate(tiles, axis=1), w_off[h], across, preferred_element_type=F32
                    )
                )
            )
        if j == ITERS - 1:
            terms.append(sum(field[h] * (2.0 * ahead[h] + near[h]) for h in range(4)))
        else:
            await_products(j)
            applied = []
            for h in range(4):
                back = spread[j, 4 * yy + h]
                for s in range(2 * Y):
                    back = back + tin[j, s, h]
                applied.append(near[h] + ahead[h] + back)
            image.append(applied)
            u.append([applied[h] * inverse[h] for h in range(4)])
            terms.append(sum(field[h] * applied[h] for h in range(4)))
            terms.append(sum(u[j + 1][h] * applied[h] for h in range(4)))

    lanes = lax.broadcasted_iota(I32, (HALF, BS), 1)
    sides = lax.broadcasted_iota(I32, (HALF, BS), 0)
    row = jnp.zeros((HALF, BS), F32)
    for index, term in enumerate(terms):
        row = jnp.where(lanes == HALF * index + sides, jnp.sum(term, axis=1, keepdims=True), row)
    row = jnp.sum(row, axis=0, keepdims=True)
    chip = (Y * xx + yy) * Z + zz
    red_a[chip] = row
    red_src[0] = row

    def send_row(source, target, stage, device):
        pltpu.make_async_remote_copy(
            src_ref=source, dst_ref=target, send_sem=red_send.at[stage], recv_sem=red_recv.at[stage],
            device_id=device, device_id_type=MESH,
        ).start()

    for dx, dy in plane:
        send_row(red_src.at[0], red_a.at[chip], 0, at(dx, dy, Z - zz))

    @pl.when(zz > 0)
    def _():
        send_row(red_src.at[0], red_a.at[chip], 0, at(0, 0, Z - zz))

    last = ITERS - 1
    await_products(last)
    applied = []
    for h in range(4):
        back = spread[last, 4 * yy + h]
        for s in range(2 * Y):
            back = back + tin[last, s, h]
        applied.append(near[h] + ahead[h] + back)
    image.append(applied)

    @pl.when(zz == 0)
    def _():
        await_bytes(red_recv.at[0], red_a.at[pl.ds(0, X * Y * Z - 1)])
        values = [red_a[i] for i in range(X * Y * Z)]
        while len(values) > 1:
            values = [values[i] + values[i + 1] for i in range(0, len(values), 2)]
        red_b[0] = values[0]
        red_src[1] = values[0]
        for dz in range(1, Z):
            send_row(red_src.at[1], red_b.at[0], 1, at(0, 0, dz))

    @pl.when(zz > 0)
    def _():
        await_bytes(red_recv.at[1], red_b)

    row = red_b[0]
    gram = [
        jnp.broadcast_to(
            jnp.sum(jnp.where(lanes == HALF * i + sides, row, 0.0), axis=1, keepdims=True), (HALF, BS)
        )
        for i in range(2 * ITERS)
    ]

    def inner(a, b):
        value = None
        for i in range(len(a)):
            for k in range(len(b)):
                if a[i] is not None and b[k] is not None:
                    term = a[i] * b[k] * gram[i + k]
                    value = term if value is None else value + term
        return value

    def plus(a, b):
        return a if b is None else b if a is None else a + b

    one = jnp.ones((HALF, BS), F32)
    zc, pc, xc = [one, None, None, None], [one, None, None], [None, None, None]
    rho = gram[0]
    for step in range(ITERS):
        ac = [pc[0], plus(pc[1], pc[0]), plus(pc[2], pc[1]), pc[2]]
        alpha = rho / inner(pc, ac)
        xc = [plus(xc[i], None if pc[i] is None else alpha * pc[i]) for i in range(3)]
        zc = [plus(zc[i], None if ac[i] is None else -alpha * ac[i]) for i in range(4)]
        if step < ITERS - 1:
            fresh = inner(zc, zc)
            beta = fresh / rho
            pc = [plus(zc[i], None if pc[i] is None else beta * pc[i]) for i in range(3)]
            rho = fresh

    for h in range(4):
        outs[0, h] = xc[0] * u[0][h] + xc[1] * u[1][h] + xc[2] * u[2][h]
        outs[1, h] = zc[0] * rhs[h] + zc[1] * image[0][h] + zc[2] * image[1][h] + zc[3] * image[2][h]

    mine_half = pl.ds(HALF * core, HALF)
    ends = []
    for i in range(2):
        ends.append(to_partner(5 + i, outs.at[i, theirs], out_ref.at[i, :, mine_half]))
        keep = pltpu.make_async_copy(outs.at[i, own], out_ref.at[i, :, mine_half], local_sems.at[5 + i])
        keep.start()
        ends.append(keep)
    for j in range(ITERS):
        await_sends(j)
    await_bytes(red_send.at[0], red_a.at[pl.ds(0, X * Y - 1)])

    @pl.when(zz > 0)
    def _():
        await_bytes(red_send.at[0], red_b)

    @pl.when(zz == 0)
    def _():
        await_bytes(red_send.at[1], red_a.at[pl.ds(0, Z - 1)])

    for copy in pair:
        copy.wait_send()
    for copy in ends:
        copy.wait()


def local(right_side, diag_blocks, block_values, block_cols, block_count, cell_diagonal):
    hbm = pl.BlockSpec(memory_space=pl.ANY)
    both = pl.pallas_call(
        kernel,
        out_shape=jax.ShapeDtypeStruct((2, *right_side.shape), F32),
        in_specs=[hbm] * 5,
        out_specs=hbm,
        scratch_shapes=[
            pltpu.VMEM((4, HALF, BS), F32),
            pltpu.VMEM((4, HALF, BS), F32),
            pltpu.VMEM((2, BS, BS), F32),
            pltpu.VMEM((2, BS), F32),
            pltpu.VMEM((4, BS, BS), F32),
            pltpu.VMEM((4, K, BS, BS), F32),
            pltpu.VMEM((2, 2, K), I32),
            pltpu.SMEM((4 * K,), I32),
            pltpu.SMEM((4 * 2 * GROUP,), I32),
            pltpu.VMEM((4, 2 * BS, K * BS), BF16),
            pltpu.VMEM((4, 2 * BS, BS), BF16),
            pltpu.VMEM((ITERS, 4, HALF, BS), F32),
            pltpu.VMEM((2 * GROUP + 1, HALF, BS), F32),
            pltpu.VMEM((2 * GROUP + 1, HALF, BS), F32),
            pltpu.VMEM((2 * GROUP + 1, HALF, BS), F32),
            pltpu.VMEM((4 * (K + 1), HALF, BS), F32),
            pltpu.VMEM((ITERS, 2 * GROUP, HALF, BS), F32),
            pltpu.VMEM((ITERS, 2 * Y, 4, HALF, BS), F32),
            pltpu.VMEM((2, 1, BS), F32),
            pltpu.VMEM((X * Y * Z, 1, BS), F32),
            pltpu.VMEM((1, 1, BS), F32),
            pltpu.VMEM((2, 4, HALF, BS), F32),
            pltpu.SemaphoreType.DMA((7,)),
            pltpu.SemaphoreType.DMA((7,)),
            pltpu.SemaphoreType.DMA((7,)),
            pltpu.SemaphoreType.DMA((ITERS, 4)),
            pltpu.SemaphoreType.DMA((ITERS, 4)),
            pltpu.SemaphoreType.DMA((2,)),
            pltpu.SemaphoreType.DMA((2,)),
            pltpu.SemaphoreType.REGULAR((4,)),
        ],
        compiler_params=pltpu.CompilerParams(
            collective_id=0, has_side_effects=True, vmem_limit_bytes=60 << 20
        ),
        name="cg",
    )(right_side, diag_blocks, block_values, block_cols, cell_diagonal)
    return both[0], both[1]


def solution(mesh):
    rows = P(("dom", "sub"))
    return jax.shard_map(
        local,
        mesh=mesh,
        in_specs=(rows,) * 6,
        out_specs=(rows, rows),
        check_vma=False,
    )
```

```python
import functools

import jax
import jax.numpy as jnp
from jax import lax
from jax.experimental import pallas as pl
from jax.experimental.pallas import tpu as pltpu
from jax.sharding import PartitionSpec as P

MESH = pl.DeviceIdType.MESH
K = 4
ITERS = 3
BS = 128
HALF = 8
X, Y, Z = 4, 4, 16
N_DOM = X * Z
GROUP = 4 * Y
F32, BF16, I32 = jnp.float32, jnp.bfloat16, jnp.int32


def ring_order(n):
    return sorted(range(1, n), key=lambda d: -min(d, n - d))


def split(v):
    high = v.astype(BF16).astype(F32)
    return jnp.concatenate([high, v - high], axis=0).astype(BF16)


def kernel(
    right_ref, diag_ref, blocks_ref, cols_ref, celld_ref, out_ref,
    rhs, dst, diag_in, dcell, sym, blocks, cols_v, place_s, slot_s, w_off, w_sym,
    mine, win_0, win_1, win_2, prods, spread, tin, red_src, red_a, red_b, outs,
    local_sems, pair_send, pair_recv, ex_send, ex_recv, red_send, red_recv, meet,
):
    dom, sub = lax.axis_index("dom"), lax.axis_index("sub")
    xx, zz = dom // Z, lax.rem(dom, Z)
    yy, core = sub // 2, lax.rem(sub, 2)
    other = 1 - core
    own = pl.ds(2 * core, 2)
    theirs = pl.ds(2 * other, 2)
    partner = (dom, 2 * yy + other)

    def at(dx, dy, dz):
        return (
            lax.rem(xx + dx, X) * Z + lax.rem(zz + dz, Z),
            2 * lax.rem(yy + dy, Y) + core,
        )

    def dom_at(step, dy):
        return (lax.rem(dom + step + N_DOM, N_DOM), 2 * lax.rem(yy + dy, Y) + core)

    loads = [
        pltpu.make_async_copy(celld_ref, dcell, local_sems.at[0]),
        pltpu.make_async_copy(right_ref.at[:, pl.ds(HALF * core, HALF)], rhs.at[own], local_sems.at[1]),
        pltpu.make_async_copy(diag_ref, diag_in, local_sems.at[2]),
        pltpu.make_async_copy(blocks_ref, blocks.at[own], local_sems.at[3]),
        pltpu.make_async_copy(cols_ref, cols_v.at[core], local_sems.at[4]),
    ]
    for load in loads:
        load.start()

    win = (win_0, win_1, win_2)
    for window in win:
        window[...] = jnp.zeros_like(window)
    tin[...] = jnp.zeros_like(tin)

    barrier = pltpu.get_barrier_semaphore()
    plane = [(dx, dy) for dx in range(X) for dy in range(Y) if dx or dy]
    plane.sort(key=lambda p: -(min(p[0], X - p[0]) + min(p[1], Y - p[1])))
    greet = [dom_at(step, dy) for dy in (2, 1, 3, 0) for step in (1, -1)]
    greet += [at(0, 0, dz) for dz in (1, 2, Z - 2, Z - 1)]
    greet += [at(dx, dy, 0) for dx, dy in plane]

    @pl.when(core == 0)
    def _():
        pl.semaphore_signal(barrier, inc=1, device_id=partner, device_id_type=MESH)

    for to_dom, to_sub in greet:
        pl.semaphore_signal(
            barrier, inc=1, device_id=(to_dom, to_sub - core), device_id_type=MESH
        )

    def to_partner(index, source, target):
        copy = pltpu.make_async_remote_copy(
            src_ref=source, dst_ref=target, send_sem=pair_send.at[index], recv_sem=pair_recv.at[index],
            device_id=partner, device_id_type=MESH,
        )
        copy.start()
        return copy

    @pl.when(core == 1)
    def _():
        pl.semaphore_wait(barrier, 1)
        pl.semaphore_signal(meet.at[0], inc=1, device_id=partner, device_id_type=MESH)

    @pl.when(core == 0)
    def _():
        pl.semaphore_wait(meet.at[0], 1)

    pair = [
        to_partner(0, right_ref.at[:, pl.ds(HALF * other, HALF)], rhs.at[own]),
        to_partner(2, cols_ref, cols_v.at[core]),
        to_partner(3, blocks_ref, blocks.at[own]),
    ]

    for h in range(4):
        prods[5 * h + K] = jnp.zeros((HALF, BS), F32)
    def tabulate(which):
        base = 2 * which
        columns = cols_v[which]
        places = [columns[i, k] for i in range(2) for k in range(K)]
        places = [jnp.where(place > 0, place, 2 * GROUP) for place in places]
        for i in range(2):
            for k in range(K):
                place_s[(base + i) * K + k] = places[i * K + k]
            for w in range(2 * GROUP):
                slot = K
                for k in range(K):
                    slot = jnp.where(places[i * K + k] == w, k, slot)
                slot_s[(base + i) * 2 * GROUP + w] = slot + (base + i) * (K + 1)

    loads[4].wait()
    tabulate(core)

    def widen(h):
        for k in range(K):
            block = blocks[h, k]
            high = block.astype(BF16)
            w_off[h, 0:BS, k * BS : (k + 1) * BS] = high
            w_off[h, BS : 2 * BS, k * BS : (k + 1) * BS] = (block - high.astype(F32)).astype(BF16)

    def widen_sym(h):
        high = sym[h].astype(BF16)
        w_sym[h, 0:BS, :] = high
        w_sym[h, BS : 2 * BS, :] = (sym[h] - high.astype(F32)).astype(BF16)

    loads[0].wait()
    for i in range(2):
        dst[2 * core + i] = jnp.broadcast_to(dcell[i : i + 1, :], (HALF, BS))
    pair.insert(1, to_partner(1, dst.at[own], dst.at[own]))
    loads[2].wait()
    upper = lax.broadcasted_iota(I32, (BS, BS), 0) < lax.broadcasted_iota(I32, (BS, BS), 1)
    for i in range(2):
        part = jnp.where(upper, diag_in[i], 0.0)
        sym[2 * core + i] = part + part.T
    pair.append(to_partner(4, sym.at[own], sym.at[own]))
    loads[3].wait()
    for i in range(2):
        widen(2 * core + i)
    pair[2].wait_recv()
    tabulate(other)

    @pl.when(core == 0)
    def _():
        pl.semaphore_wait(barrier, 2 * len(greet))
        pl.semaphore_signal(meet.at[0], inc=1, device_id=partner, device_id_type=MESH)

    @pl.when(core == 1)
    def _():
        pl.semaphore_wait(meet.at[0], 1)

    reach = ((1, 2, Z - 2, Z - 1), (4, Z - 4), (6, Z - 6))

    def hail(step):
        for dz in reach[step]:
            pl.semaphore_signal(meet.at[step + 1], inc=1, device_id=at(0, 0, dz), device_id_type=MESH)

    hail(0)

    loads[1].wait()
    pair[0].wait_recv()
    pair[1].wait_recv()
    inverse = [1.0 / dst[h] for h in range(4)]
    u = [[rhs[h] * inverse[h] for h in range(4)]]
    image = []

    def exchange(index, j, source, target, device):
        return pltpu.make_async_remote_copy(
            src_ref=source, dst_ref=target, send_sem=ex_send.at[j, index], recv_sem=ex_recv.at[j, index],
            device_id=device, device_id_type=MESH,
        )

    def await_bytes(sem, buffer):
        pltpu.make_async_copy(buffer, buffer, sem).wait()

    def send_field_back(j, order):
        @pl.when(dom > 0)
        def _():
            for dy in order:
                exchange(0, j, mine.at[j], win[j].at[pl.ds(GROUP + 4 * yy, 4)], dom_at(-1, dy)).start()

    def send_field_own(j):
        for y_here in range(1, Y):
            @pl.when(yy == y_here)
            def _():
                for y_there in range(y_here):
                    exchange(
                        1, j, mine.at[j], win[j].at[pl.ds(4 * y_here, 4)], (dom, 2 * y_there + core)
                    ).start()

    def send_products_on(j, order):
        @pl.when(dom < N_DOM - 1)
        def _():
            for dy in order:
                rows = pl.ds(GROUP + 4 * lax.rem(yy + dy, Y), 4)
                exchange(2, j, spread.at[j, rows], tin.at[j, Y + yy], dom_at(1, dy)).start()

    def send_products_own(j):
        for y_here in range(Y - 1):
            @pl.when(yy == y_here)
            def _():
                for y_there in range(y_here + 1, Y):
                    exchange(
                        3, j, spread.at[j, pl.ds(4 * y_there, 4)], tin.at[j, y_here], (dom, 2 * y_there + core)
                    ).start()

    def await_field(j):
        for y_here in range(Y - 1):
            @pl.when(yy == y_here)
            def _():
                await_bytes(ex_recv.at[j, 1], win[j].at[pl.ds(0, 4 * (Y - 1 - y_here))])

        @pl.when(dom < N_DOM - 1)
        def _():
            await_bytes(ex_recv.at[j, 0], win[j].at[pl.ds(GROUP, GROUP)])

    def await_products(j):
        for y_here in range(1, Y):
            @pl.when(yy == y_here)
            def _():
                await_bytes(ex_recv.at[j, 3], win[j].at[pl.ds(0, 4 * y_here)])

        @pl.when(dom > 0)
        def _():
            await_bytes(ex_recv.at[j, 2], win[j].at[pl.ds(GROUP, GROUP)])

    def await_sends(j):
        @pl.when(dom > 0)
        def _():
            await_bytes(ex_send.at[j, 0], win[j].at[pl.ds(GROUP, GROUP)])

        @pl.when(dom < N_DOM - 1)
        def _():
            await_bytes(ex_send.at[j, 2], win[j].at[pl.ds(GROUP, GROUP)])

        for y_here in range(Y):
            @pl.when(yy == y_here)
            def _():
                if y_here:
                    await_bytes(ex_send.at[j, 1], win[j].at[pl.ds(0, 4 * y_here)])
                if y_here < Y - 1:
                    await_bytes(ex_send.at[j, 3], win[j].at[pl.ds(0, 4 * (Y - 1 - y_here))])

    def fold(out):
        return (out[0:HALF, 0:BS] + out[0:HALF, BS:]) + (out[HALF:, 0:BS] + out[HALF:, BS:])

    lanes = lax.broadcasted_iota(I32, (HALF, BS), 1)
    sides = lax.broadcasted_iota(I32, (HALF, BS), 0)

    def in_row(first, terms):
        values = jnp.zeros((HALF, BS), F32)
        for index, term in enumerate(terms):
            place = HALF * (first + index) + sides
            values = jnp.where(lanes == place, jnp.sum(term, axis=1, keepdims=True), values)
        return values

    across = (((1,), (1,)), ((), ()))
    terms = []
    terms.append(sum(rhs[h] * u[0][h] for h in range(4)))

    for j in range(ITERS):
        field = u[j]
        for h in range(4):
            mine[j, h] = field[h]
            win[j][4 * yy + h] = field[h]
        send_field_back(j, (2,))
        parts = [split(field[h]) for h in range(4)]
        if j == 0:
            pair[3].wait_recv()
            for i in range(2):
                widen(2 * other + i)
        for h in range(4):
            out = jnp.dot(
                jnp.concatenate([parts[h], parts[h]], axis=1), w_off[h], preferred_element_type=F32
            )
            for k in range(K):
                prods[5 * h + k] = out[0:HALF, k * BS : (k + 1) * BS] + out[HALF:, k * BS : (k + 1) * BS]

        def gather_products(first):
            for w in range(first, first + GROUP):
                picked = [prods[slot_s[h * 2 * GROUP + w]] for h in range(4)]
                spread[j, w] = (picked[0] + picked[1]) + (picked[2] + picked[3])

        gather_products(GROUP)
        send_products_on(j, (2,))
        send_field_back(j, (1, 3))
        send_products_on(j, (1, 3))
        send_field_own(j)
        gather_products(0)
        send_products_own(j)
        send_field_back(j, (0,))
        send_products_on(j, (0,))
        if j == 0:
            pair[4].wait_recv()
            for h in range(4):
                widen_sym(h)
        near = [
            fold(lax.dot_general(parts[h], w_sym[h], across, preferred_element_type=F32)) for h in range(4)
        ]
        if j == ITERS - 1:
            row = in_row(0, terms)
            await_field(j)
            pl.semaphore_wait(meet.at[j + 1], len(reach[j]))
        else:
            pl.semaphore_wait(meet.at[j + 1], len(reach[j]))
            hail(j + 1)
            await_field(j)
        ahead = []
        for h in range(4):
            tiles = [split(win[j][place_s[h * K + k]]) for k in range(K)]
            ahead.append(
                fold(
                    lax.dot_general(
                        jnp.concatenate(tiles, axis=1), w_off[h], across, preferred_element_type=F32
                    )
                )
            )
        if j == ITERS - 1:
            terms.append(sum(field[h] * (2.0 * ahead[h] + near[h]) for h in range(4)))
        else:
            await_products(j)
            applied = []
            for h in range(4):
                back = spread[j, 4 * yy + h]
                for s in range(2 * Y):
                    back = back + tin[j, s, h]
                applied.append(near[h] + ahead[h] + back)
            image.append(applied)
            u.append([applied[h] * inverse[h] for h in range(4)])
            terms.append(sum(field[h] * applied[h] for h in range(4)))
            terms.append(sum(u[j + 1][h] * applied[h] for h in range(4)))

    row = jnp.sum(row + in_row(2 * ITERS - 1, terms[2 * ITERS - 1 :]), axis=0, keepdims=True)
    chip = (Y * xx + yy) * Z + zz
    red_a[chip] = row
    red_src[0] = row

    def send_row(source, target, stage, device):
        pltpu.make_async_remote_copy(
            src_ref=source, dst_ref=target, send_sem=red_send.at[stage], recv_sem=red_recv.at[stage],
            device_id=device, device_id_type=MESH,
        ).start()

    for z_root in range(2):
        for dx, dy in plane:
            send_row(red_src.at[0], red_a.at[chip], 0, at(dx, dy, Z + z_root - zz))

        @pl.when(zz != z_root)
        def _():
            send_row(red_src.at[0], red_a.at[chip], 0, at(0, 0, Z + z_root - zz))

    last = ITERS - 1
    await_products(last)
    applied = []
    for h in range(4):
        back = spread[last, 4 * yy + h]
        for s in range(2 * Y):
            back = back + tin[last, s, h]
        applied.append(near[h] + ahead[h] + back)
    image.append(applied)

    @pl.when(zz < 2)
    def _():
        await_bytes(red_recv.at[0], red_a.at[pl.ds(0, X * Y * Z - 1)])
        values = [red_a[i] for i in range(X * Y * Z)]
        while len(values) > 1:
            values = [values[i] + values[i + 1] for i in range(0, len(values), 2)]
        red_b[0] = values[0]
        red_src[1] = values[0]

    @pl.when(zz == 1)
    def _():
        for dz in range(1, 8):
            send_row(red_src.at[1], red_b.at[0], 1, at(0, 0, dz))

    @pl.when(zz == 0)
    def _():
        for dz in range(9, 16):
            send_row(red_src.at[1], red_b.at[0], 1, at(0, 0, dz))

    @pl.when(zz > 1)
    def _():
        await_bytes(red_recv.at[1], red_b)

    row = red_b[0]
    gram = [
        jnp.broadcast_to(
            jnp.sum(jnp.where(lanes == HALF * i + sides, row, 0.0), axis=1, keepdims=True), (HALF, BS)
        )
        for i in range(2 * ITERS)
    ]

    def inner(a, b):
        value = None
        for i in range(len(a)):
            for k in range(len(b)):
                if a[i] is not None and b[k] is not None:
                    term = a[i] * b[k] * gram[i + k]
                    value = term if value is None else value + term
        return value

    def plus(a, b):
        return a if b is None else b if a is None else a + b

    one = jnp.ones((HALF, BS), F32)
    zc, pc, xc = [one, None, None, None], [one, None, None], [None, None, None]
    rho = gram[0]
    for step in range(ITERS):
        ac = [pc[0], plus(pc[1], pc[0]), plus(pc[2], pc[1]), pc[2]]
        alpha = rho / inner(pc, ac)
        xc = [plus(xc[i], None if pc[i] is None else alpha * pc[i]) for i in range(3)]
        zc = [plus(zc[i], None if ac[i] is None else -alpha * ac[i]) for i in range(4)]
        if step < ITERS - 1:
            fresh = inner(zc, zc)
            beta = fresh / rho
            pc = [plus(zc[i], None if pc[i] is None else beta * pc[i]) for i in range(3)]
            rho = fresh

    for h in range(4):
        outs[0, h] = xc[0] * u[0][h] + xc[1] * u[1][h] + xc[2] * u[2][h]
        outs[1, h] = zc[0] * rhs[h] + zc[1] * image[0][h] + zc[2] * image[1][h] + zc[3] * image[2][h]

    mine_half = pl.ds(HALF * core, HALF)
    ends = []
    for i in range(2):
        ends.append(to_partner(5 + i, outs.at[i, theirs], out_ref.at[i, :, mine_half]))
        keep = pltpu.make_async_copy(outs.at[i, own], out_ref.at[i, :, mine_half], local_sems.at[5 + i])
        keep.start()
        ends.append(keep)
    for j in range(ITERS):
        await_sends(j)
    await_bytes(red_send.at[0], red_a.at[pl.ds(0, 2 * X * Y - 1)])

    @pl.when(zz > 1)
    def _():
        await_bytes(red_send.at[0], red_b)

    @pl.when(zz < 2)
    def _():
        await_bytes(red_send.at[1], red_a.at[pl.ds(0, 7)])

    for copy in pair:
        copy.wait_send()
    for copy in ends:
        copy.wait()


def local(right_side, diag_blocks, block_values, block_cols, block_count, cell_diagonal):
    hbm = pl.BlockSpec(memory_space=pl.ANY)
    both = pl.pallas_call(
        kernel,
        out_shape=jax.ShapeDtypeStruct((2, *right_side.shape), F32),
        in_specs=[hbm] * 5,
        out_specs=hbm,
        scratch_shapes=[
            pltpu.VMEM((4, HALF, BS), F32),
            pltpu.VMEM((4, HALF, BS), F32),
            pltpu.VMEM((2, BS, BS), F32),
            pltpu.VMEM((2, BS), F32),
            pltpu.VMEM((4, BS, BS), F32),
            pltpu.VMEM((4, K, BS, BS), F32),
            pltpu.VMEM((2, 2, K), I32),
            pltpu.SMEM((4 * K,), I32),
            pltpu.SMEM((4 * 2 * GROUP,), I32),
            pltpu.VMEM((4, 2 * BS, K * BS), BF16),
            pltpu.VMEM((4, 2 * BS, BS), BF16),
            pltpu.VMEM((ITERS, 4, HALF, BS), F32),
            pltpu.VMEM((2 * GROUP + 1, HALF, BS), F32),
            pltpu.VMEM((2 * GROUP + 1, HALF, BS), F32),
            pltpu.VMEM((2 * GROUP + 1, HALF, BS), F32),
            pltpu.VMEM((4 * (K + 1), HALF, BS), F32),
            pltpu.VMEM((ITERS, 2 * GROUP, HALF, BS), F32),
            pltpu.VMEM((ITERS, 2 * Y, 4, HALF, BS), F32),
            pltpu.VMEM((2, 1, BS), F32),
            pltpu.VMEM((X * Y * Z, 1, BS), F32),
            pltpu.VMEM((1, 1, BS), F32),
            pltpu.VMEM((2, 4, HALF, BS), F32),
            pltpu.SemaphoreType.DMA((7,)),
            pltpu.SemaphoreType.DMA((7,)),
            pltpu.SemaphoreType.DMA((7,)),
            pltpu.SemaphoreType.DMA((ITERS, 4)),
            pltpu.SemaphoreType.DMA((ITERS, 4)),
            pltpu.SemaphoreType.DMA((2,)),
            pltpu.SemaphoreType.DMA((2,)),
            pltpu.SemaphoreType.REGULAR((4,)),
        ],
        compiler_params=pltpu.CompilerParams(
            collective_id=0, has_side_effects=True, vmem_limit_bytes=60 << 20
        ),
        name="cg",
    )(right_side, diag_blocks, block_values, block_cols, cell_diagonal)
    return both[0], both[1]


def solution(mesh):
    rows = P(("dom", "sub"))
    return jax.shard_map(
        local,
        mesh=mesh,
        in_specs=(rows,) * 6,
        out_specs=(rows, rows),
        check_vma=False,
    )
```

```python
import functools

import jax
import jax.numpy as jnp
from jax import lax
from jax.experimental import pallas as pl
from jax.experimental.pallas import tpu as pltpu
from jax.sharding import PartitionSpec as P

MESH = pl.DeviceIdType.MESH
K = 4
ITERS = 3
BS = 128
HALF = 8
X, Y, Z = 4, 4, 16
N_DOM = X * Z
GROUP = 4 * Y
SIDE = 64
FAR = range(6, 11)
F32, BF16, I32 = jnp.float32, jnp.bfloat16, jnp.int32


def ring_order(n):
    return sorted(range(1, n), key=lambda d: -min(d, n - d))


def split(v):
    high = v.astype(BF16).astype(F32)
    return jnp.concatenate([high, v - high], axis=0).astype(BF16)


def kernel(
    right_ref, diag_ref, blocks_ref, cols_ref, celld_ref, out_ref,
    rhs, rhs_all, image, image_in, dst, diag_in, dcell, sym, blocks, cols_v, place_s, slot_s, w_off, w_sym,
    mine, win_0, win_1, win_2, prods, spread, tin, red_src, red_a, red_b, red_c, outs,
    local_sems, pair_send, pair_recv, ex_send, ex_recv, red_send, red_recv, meet,
):
    dom, sub = lax.axis_index("dom"), lax.axis_index("sub")
    xx, zz = dom // Z, lax.rem(dom, Z)
    yy, core = sub // 2, lax.rem(sub, 2)
    other = 1 - core
    own = pl.ds(2 * core, 2)
    theirs = pl.ds(2 * other, 2)
    partner = (dom, 2 * yy + other)

    def at(dx, dy, dz):
        return (
            lax.rem(xx + dx, X) * Z + lax.rem(zz + dz, Z),
            2 * lax.rem(yy + dy, Y) + core,
        )

    def dom_at(step, dy):
        return (lax.rem(dom + step + N_DOM, N_DOM), 2 * lax.rem(yy + dy, Y) + core)

    loads = [
        pltpu.make_async_copy(celld_ref, dcell, local_sems.at[0]),
        pltpu.make_async_copy(right_ref.at[:, pl.ds(HALF * core, HALF)], rhs.at[own], local_sems.at[1]),
        pltpu.make_async_copy(diag_ref, diag_in, local_sems.at[2]),
        pltpu.make_async_copy(blocks_ref, blocks.at[own], local_sems.at[3]),
        pltpu.make_async_copy(cols_ref, cols_v.at[core], local_sems.at[4]),
    ]
    loads.append(pltpu.make_async_copy(right_ref, rhs_all, local_sems.at[5]))
    for load in loads:
        load.start()

    win = (win_0, win_1, win_2)
    for window in win:
        window[...] = jnp.zeros_like(window)
    tin[...] = jnp.zeros_like(tin)

    barrier = pltpu.get_barrier_semaphore()
    plane = [(dx, dy) for dx in range(X) for dy in range(Y) if dx or dy]
    plane.sort(key=lambda p: -(min(p[0], X - p[0]) + min(p[1], Y - p[1])))
    greet = [dom_at(step, dy) for dy in (2, 1, 3, 0) for step in (1, -1)]
    greet += [at(0, 0, dz) for dz in (1, 2, Z - 2, Z - 1)]
    greet += [at(dx, dy, 0) for dx, dy in plane]

    @pl.when(core == 0)
    def _():
        pl.semaphore_signal(barrier, inc=1, device_id=partner, device_id_type=MESH)

    for to_dom, to_sub in greet:
        pl.semaphore_signal(
            barrier, inc=1, device_id=(to_dom, to_sub - core), device_id_type=MESH
        )

    def to_partner(index, source, target):
        copy = pltpu.make_async_remote_copy(
            src_ref=source, dst_ref=target, send_sem=pair_send.at[index], recv_sem=pair_recv.at[index],
            device_id=partner, device_id_type=MESH,
        )
        copy.start()
        return copy

    @pl.when(core == 1)
    def _():
        pl.semaphore_wait(barrier, 1)
        pl.semaphore_signal(meet.at[0], inc=1, device_id=partner, device_id_type=MESH)

    @pl.when(core == 0)
    def _():
        pl.semaphore_wait(meet.at[0], 1)

    pair = [
        to_partner(0, right_ref.at[:, pl.ds(HALF * other, HALF)], rhs.at[own]),
        to_partner(2, cols_ref, cols_v.at[core]),
        to_partner(3, blocks_ref, blocks.at[own]),
    ]

    for h in range(4):
        prods[5 * h + K] = jnp.zeros((HALF, BS), F32)
    def tabulate(which):
        base = 2 * which
        columns = cols_v[which]
        places = [columns[i, k] for i in range(2) for k in range(K)]
        places = [jnp.where(place > 0, place, 2 * GROUP) for place in places]
        for i in range(2):
            for k in range(K):
                place_s[(base + i) * K + k] = places[i * K + k]
            for w in range(2 * GROUP):
                slot = K
                for k in range(K):
                    slot = jnp.where(places[i * K + k] == w, k, slot)
                slot_s[(base + i) * 2 * GROUP + w] = slot + (base + i) * (K + 1)

    loads[4].wait()
    tabulate(core)

    def widen(h):
        for k in range(K):
            block = blocks[h, k]
            high = block.astype(BF16)
            w_off[h, 0:BS, k * BS : (k + 1) * BS] = high
            w_off[h, BS : 2 * BS, k * BS : (k + 1) * BS] = (block - high.astype(F32)).astype(BF16)

    def widen_sym(h):
        high = sym[h].astype(BF16)
        w_sym[h, 0:BS, :] = high
        w_sym[h, BS : 2 * BS, :] = (sym[h] - high.astype(F32)).astype(BF16)

    loads[0].wait()
    for i in range(2):
        dst[2 * core + i] = jnp.broadcast_to(dcell[i : i + 1, :], (HALF, BS))
    pair.insert(1, to_partner(1, dst.at[own], dst.at[own]))
    loads[2].wait()
    upper = lax.broadcasted_iota(I32, (BS, BS), 0) < lax.broadcasted_iota(I32, (BS, BS), 1)
    for i in range(2):
        part = jnp.where(upper, diag_in[i], 0.0)
        sym[2 * core + i] = part + part.T
    pair.append(to_partner(4, sym.at[own], sym.at[own]))
    loads[3].wait()
    for i in range(2):
        widen(2 * core + i)
    pair[2].wait_recv()
    tabulate(other)

    @pl.when(core == 0)
    def _():
        pl.semaphore_wait(barrier, 2 * len(greet))
        pl.semaphore_signal(meet.at[0], inc=1, device_id=partner, device_id_type=MESH)

    @pl.when(core == 1)
    def _():
        pl.semaphore_wait(meet.at[0], 1)

    reach = ((1, 2, Z - 2, Z - 1), (4, Z - 4), (6, Z - 6))

    def hail(step):
        for dz in reach[step]:
            pl.semaphore_signal(meet.at[step + 1], inc=1, device_id=at(0, 0, dz), device_id_type=MESH)

    hail(0)

    loads[1].wait()
    pair[0].wait_recv()
    pair[1].wait_recv()
    inverse = [1.0 / dst[h] for h in range(4)]
    u = [[rhs[h] * inverse[h] for h in range(4)]]

    def exchange(index, j, source, target, device):
        return pltpu.make_async_remote_copy(
            src_ref=source, dst_ref=target, send_sem=ex_send.at[j, index], recv_sem=ex_recv.at[j, index],
            device_id=device, device_id_type=MESH,
        )

    def await_bytes(sem, buffer):
        pltpu.make_async_copy(buffer, buffer, sem).wait()

    def send_field_back(j, order):
        @pl.when(dom > 0)
        def _():
            for dy in order:
                exchange(0, j, mine.at[j], win[j].at[pl.ds(GROUP + 4 * yy, 4)], dom_at(-1, dy)).start()

    def send_field_own(j):
        for y_here in range(1, Y):
            @pl.when(yy == y_here)
            def _():
                for y_there in range(y_here):
                    exchange(
                        1, j, mine.at[j], win[j].at[pl.ds(4 * y_here, 4)], (dom, 2 * y_there + core)
                    ).start()

    def send_products_on(j, order):
        @pl.when(dom < N_DOM - 1)
        def _():
            for dy in order:
                rows = pl.ds(GROUP + 4 * lax.rem(yy + dy, Y), 4)
                exchange(2, j, spread.at[j, rows], tin.at[j, Y + yy], dom_at(1, dy)).start()

    def send_products_own(j):
        for y_here in range(Y - 1):
            @pl.when(yy == y_here)
            def _():
                for y_there in range(y_here + 1, Y):
                    exchange(
                        3, j, spread.at[j, pl.ds(4 * y_there, 4)], tin.at[j, y_here], (dom, 2 * y_there + core)
                    ).start()

    def await_field(j):
        for y_here in range(Y - 1):
            @pl.when(yy == y_here)
            def _():
                await_bytes(ex_recv.at[j, 1], win[j].at[pl.ds(0, 4 * (Y - 1 - y_here))])

        @pl.when(dom < N_DOM - 1)
        def _():
            await_bytes(ex_recv.at[j, 0], win[j].at[pl.ds(GROUP, GROUP)])

    def await_products(j):
        for y_here in range(1, Y):
            @pl.when(yy == y_here)
            def _():
                await_bytes(ex_recv.at[j, 3], win[j].at[pl.ds(0, 4 * y_here)])

        @pl.when(dom > 0)
        def _():
            await_bytes(ex_recv.at[j, 2], win[j].at[pl.ds(GROUP, GROUP)])

    def await_sends(j):
        @pl.when(dom > 0)
        def _():
            await_bytes(ex_send.at[j, 0], win[j].at[pl.ds(GROUP, GROUP)])

        @pl.when(dom < N_DOM - 1)
        def _():
            await_bytes(ex_send.at[j, 2], win[j].at[pl.ds(GROUP, GROUP)])

        for y_here in range(Y):
            @pl.when(yy == y_here)
            def _():
                if y_here:
                    await_bytes(ex_send.at[j, 1], win[j].at[pl.ds(0, 4 * y_here)])
                if y_here < Y - 1:
                    await_bytes(ex_send.at[j, 3], win[j].at[pl.ds(0, 4 * (Y - 1 - y_here))])

    def fold(out):
        return (out[0:HALF, 0:BS] + out[0:HALF, BS:]) + (out[HALF:, 0:BS] + out[HALF:, BS:])

    lanes = lax.broadcasted_iota(I32, (HALF, BS), 1)
    sides = lax.broadcasted_iota(I32, (HALF, BS), 0)

    def in_row(first, terms):
        values = jnp.zeros((HALF, BS), F32)
        for index, term in enumerate(terms):
            place = SIDE * core + HALF * (first + index) + sides
            values = jnp.where(lanes == place, jnp.sum(term, axis=1, keepdims=True), values)
        return values

    def swap_image(j, applied):
        for h in range(4):
            image[j, h] = applied[h]
        pair.append(to_partner(5 + j, image.at[j, theirs], image_in.at[j]))

    across = (((1,), (1,)), ((), ()))
    terms = []
    terms.append(sum(rhs[h] * u[0][h] for h in range(4)))

    for j in range(ITERS):
        field = u[j]
        for h in range(4):
            mine[j, h] = field[h]
            win[j][4 * yy + h] = field[h]
        send_field_back(j, (2, 1, 3))
        send_field_own(j)
        send_field_back(j, (0,))
        parts = [split(field[h]) for h in range(4)]
        if j == 0:
            pair[3].wait_recv()
            for i in range(2):
                widen(2 * other + i)
        for h in range(4):
            out = jnp.dot(
                jnp.concatenate([parts[h], parts[h]], axis=1), w_off[h], preferred_element_type=F32
            )
            for k in range(K):
                prods[5 * h + k] = out[0:HALF, k * BS : (k + 1) * BS] + out[HALF:, k * BS : (k + 1) * BS]

        def gather_products(first):
            for w in range(first, first + GROUP):
                picked = [prods[slot_s[h * 2 * GROUP + w]] for h in range(4)]
                spread[j, w] = (picked[0] + picked[1]) + (picked[2] + picked[3])

        gather_products(GROUP)
        send_products_on(j, (2, 1, 3))
        gather_products(0)
        send_products_own(j)
        send_products_on(j, (0,))
        if j == 0:
            pair[4].wait_recv()
            for h in range(4):
                widen_sym(h)
        near = [
            fold(lax.dot_general(parts[h], w_sym[h], across, preferred_element_type=F32)) for h in range(4)
        ]
        if j == ITERS - 1:
            row = in_row(0, terms)
            await_field(j)
            pl.semaphore_wait(meet.at[j + 1], len(reach[j]))
        else:
            pl.semaphore_wait(meet.at[j + 1], len(reach[j]))
            hail(j + 1)
            await_field(j)
        ahead = []
        for h in range(4):
            tiles = [split(win[j][place_s[h * K + k]]) for k in range(K)]
            ahead.append(
                fold(
                    lax.dot_general(
                        jnp.concatenate(tiles, axis=1), w_off[h], across, preferred_element_type=F32
                    )
                )
            )
        if j == ITERS - 1:
            terms.append(sum(field[h] * (2.0 * ahead[h] + near[h]) for h in range(4)))
        else:
            await_products(j)
            applied = []
            for h in range(4):
                back = spread[j, 4 * yy + h]
                for s in range(2 * Y):
                    back = back + tin[j, s, h]
                applied.append(near[h] + ahead[h] + back)
            swap_image(j, applied)
            u.append([applied[h] * inverse[h] for h in range(4)])
            terms.append(sum(field[h] * applied[h] for h in range(4)))
            terms.append(sum(u[j + 1][h] * applied[h] for h in range(4)))

    row = jnp.sum(row + in_row(2 * ITERS - 1, terms[2 * ITERS - 1 :]), axis=0, keepdims=True)
    slot = (zz * Y * X + Y * xx + yy) * 2 + core
    red_a[slot] = row
    red_src[0] = row

    def send_row(source, target, stage, arrival, device):
        pltpu.make_async_remote_copy(
            src_ref=source, dst_ref=target, send_sem=red_send.at[stage], recv_sem=red_recv.at[arrival],
            device_id=device, device_id_type=MESH,
        ).start()

    arrival = jnp.where((zz >= FAR[0]) & (zz <= FAR[-1]), 1, 0)
    for dx, dy in plane:
        to_dom, to_sub = at(dx, dy, Z - zz)
        for to in (to_sub, to_sub + 1 - 2 * core):
            send_row(red_src.at[0], red_a.at[slot], 0, arrival, (to_dom, to))
    to_dom, to_sub = at(0, 0, Z - zz)
    send_row(red_src.at[0], red_a.at[slot], 0, arrival, (to_dom, to_sub + 1 - 2 * core))

    @pl.when(zz > 0)
    def _():
        send_row(red_src.at[0], red_a.at[slot], 0, arrival, (to_dom, to_sub))

    for dx, dy in plane:
        send_row(red_src.at[0], red_a.at[slot], 0, arrival, at(dx, dy, Z + 1 - zz))

    @pl.when(zz != 1)
    def _():
        send_row(red_src.at[0], red_a.at[slot], 0, arrival, at(0, 0, Z + 1 - zz))

    last = ITERS - 1
    await_products(last)
    applied = []
    for h in range(4):
        back = spread[last, 4 * yy + h]
        for s in range(2 * Y):
            back = back + tin[last, s, h]
        applied.append(near[h] + ahead[h] + back)
    swap_image(ITERS - 1, applied)

    near_planes = [z for z in range(Z) if z not in FAR]

    def add_rows(planes, places):
        values = [red_a[2 * X * Y * z + i] for z in planes for i in places]
        while len(values) > 1:
            values = [sum(values[i : i + 2]) for i in range(0, len(values), 2)]
        return values[0]

    @pl.when(zz == 0)
    def _():
        await_bytes(red_recv.at[0], red_a.at[pl.ds(0, 2 * X * Y * len(near_planes) - 1)])
        near_sum = add_rows(near_planes, range(2 * X * Y))
        await_bytes(red_recv.at[1], red_a.at[pl.ds(0, 2 * X * Y * len(FAR))])
        whole = near_sum + add_rows(FAR, range(2 * X * Y))
        red_b[0] = whole
        red_src[1] = whole
        for dz in (2, *range(9, Z)):
            send_row(red_src.at[1], red_b.at[0], 1, 2, at(0, 0, dz))

    @pl.when(zz == 1)
    def _():
        places = [2 * i + core for i in range(X * Y)]
        await_bytes(red_recv.at[0], red_a.at[pl.ds(0, X * Y * len(near_planes) - 1)])
        near_sum = add_rows(near_planes, places)
        await_bytes(red_recv.at[1], red_a.at[pl.ds(0, X * Y * len(FAR))])
        whole = near_sum + add_rows(FAR, places)
        red_src[1] = whole
        swap = pltpu.make_async_remote_copy(
            src_ref=red_src.at[1], dst_ref=red_c.at[0], send_sem=red_send.at[2], recv_sem=red_recv.at[3],
            device_id=partner, device_id_type=MESH,
        )
        swap.start()
        swap.wait_recv()
        whole = whole + red_c[0]
        red_b[0] = whole
        red_src[2] = whole
        for dz in range(2, 8):
            send_row(red_src.at[2], red_b.at[0], 1, 2, at(0, 0, dz))
        swap.wait_send()

    @pl.when(zz > 1)
    def _():
        await_bytes(red_recv.at[2], red_b)

    row = red_b[0]
    lanes = lax.broadcasted_iota(I32, (2 * HALF, BS), 1)
    sides = lax.broadcasted_iota(I32, (2 * HALF, BS), 0)
    first_lane = jnp.where(sides < HALF, SIDE * core + sides, SIDE * other + sides - HALF)
    gram = [
        jnp.broadcast_to(
            jnp.sum(jnp.where(lanes == first_lane + HALF * i, row, 0.0), axis=1, keepdims=True),
            (2 * HALF, BS),
        )
        for i in range(2 * ITERS)
    ]

    def inner(a, b):
        value = None
        for i in range(len(a)):
            for k in range(len(b)):
                if a[i] is not None and b[k] is not None:
                    term = a[i] * b[k] * gram[i + k]
                    value = term if value is None else value + term
        return value

    def plus(a, b):
        return a if b is None else b if a is None else a + b

    one = jnp.ones((2 * HALF, BS), F32)
    zc, pc, xc = [one, None, None, None], [one, None, None], [None, None, None]
    rho = gram[0]
    for step in range(ITERS):
        ac = [pc[0], plus(pc[1], pc[0]), plus(pc[2], pc[1]), pc[2]]
        alpha = rho / inner(pc, ac)
        xc = [plus(xc[i], None if pc[i] is None else alpha * pc[i]) for i in range(3)]
        zc = [plus(zc[i], None if ac[i] is None else -alpha * ac[i]) for i in range(4)]
        if step < ITERS - 1:
            fresh = inner(zc, zc)
            beta = fresh / rho
            pc = [plus(zc[i], None if pc[i] is None else beta * pc[i]) for i in range(3)]
            rho = fresh

    loads[5].wait()
    for copy in pair[5:]:
        copy.wait_recv()
    mine_half, their_half = pl.ds(HALF * core, HALF), pl.ds(HALF * other, HALF)
    for i in range(2):
        h = 2 * core + i
        x, z = [c[:HALF] for c in xc], [c[:HALF] for c in zc]
        outs[0, i, mine_half, :] = x[0] * mine[0, h] + x[1] * mine[1, h] + x[2] * mine[2, h]
        outs[1, i, mine_half, :] = z[0] * rhs[h] + z[1] * image[0, h] + z[2] * image[1, h] + z[3] * image[2, h]
        x, z = [c[HALF:] for c in xc], [c[HALF:] for c in zc]
        right, back = rhs_all[i, their_half, :], 1.0 / dst[h]
        outs[0, i, their_half, :] = (
            x[0] * (right * back) + x[1] * (image_in[0, i] * back) + x[2] * (image_in[1, i] * back)
        )
        outs[1, i, their_half, :] = (
            z[0] * right + z[1] * image_in[0, i] + z[2] * image_in[1, i] + z[3] * image_in[2, i]
        )
    keep = pltpu.make_async_copy(outs, out_ref, local_sems.at[6])
    keep.start()
    for j in range(ITERS):
        await_sends(j)
    await_bytes(red_send.at[0], red_a.at[pl.ds(0, 3 * X * Y - 1)])

    @pl.when(zz > 1)
    def _():
        await_bytes(red_send.at[0], red_b)

    @pl.when(zz == 0)
    def _():
        await_bytes(red_send.at[1], red_a.at[pl.ds(0, 8)])

    @pl.when(zz == 1)
    def _():
        await_bytes(red_send.at[1], red_a.at[pl.ds(0, 6)])

    for copy in pair:
        copy.wait_send()
    keep.wait()


def local(right_side, diag_blocks, block_values, block_cols, block_count, cell_diagonal):
    hbm = pl.BlockSpec(memory_space=pl.ANY)
    both = pl.pallas_call(
        kernel,
        out_shape=jax.ShapeDtypeStruct((2, *right_side.shape), F32),
        in_specs=[hbm] * 5,
        out_specs=hbm,
        scratch_shapes=[
            pltpu.VMEM((4, HALF, BS), F32),
            pltpu.VMEM((2, 2 * HALF, BS), F32),
            pltpu.VMEM((ITERS, 4, HALF, BS), F32),
            pltpu.VMEM((ITERS, 2, HALF, BS), F32),
            pltpu.VMEM((4, HALF, BS), F32),
            pltpu.VMEM((2, BS, BS), F32),
            pltpu.VMEM((2, BS), F32),
            pltpu.VMEM((4, BS, BS), F32),
            pltpu.VMEM((4, K, BS, BS), F32),
            pltpu.VMEM((2, 2, K), I32),
            pltpu.SMEM((4 * K,), I32),
            pltpu.SMEM((4 * 2 * GROUP,), I32),
            pltpu.VMEM((4, 2 * BS, K * BS), BF16),
            pltpu.VMEM((4, 2 * BS, BS), BF16),
            pltpu.VMEM((ITERS, 4, HALF, BS), F32),
            pltpu.VMEM((2 * GROUP + 1, HALF, BS), F32),
            pltpu.VMEM((2 * GROUP + 1, HALF, BS), F32),
            pltpu.VMEM((2 * GROUP + 1, HALF, BS), F32),
            pltpu.VMEM((4 * (K + 1), HALF, BS), F32),
            pltpu.VMEM((ITERS, 2 * GROUP, HALF, BS), F32),
            pltpu.VMEM((ITERS, 2 * Y, 4, HALF, BS), F32),
            pltpu.VMEM((3, 1, BS), F32),
            pltpu.VMEM((2 * X * Y * Z, 1, BS), F32),
            pltpu.VMEM((1, 1, BS), F32),
            pltpu.VMEM((1, 1, BS), F32),
            pltpu.VMEM((2, 2, 2 * HALF, BS), F32),
            pltpu.SemaphoreType.DMA((7,)),
            pltpu.SemaphoreType.DMA((8,)),
            pltpu.SemaphoreType.DMA((8,)),
            pltpu.SemaphoreType.DMA((ITERS, 4)),
            pltpu.SemaphoreType.DMA((ITERS, 4)),
            pltpu.SemaphoreType.DMA((3,)),
            pltpu.SemaphoreType.DMA((4,)),
            pltpu.SemaphoreType.REGULAR((4,)),
        ],
        compiler_params=pltpu.CompilerParams(
            collective_id=0, has_side_effects=True, vmem_limit_bytes=60 << 20
        ),
        name="cg",
    )(right_side, diag_blocks, block_values, block_cols, cell_diagonal)
    return both[0], both[1]


def solution(mesh):
    rows = P(("dom", "sub"))
    return jax.shard_map(
        local,
        mesh=mesh,
        in_specs=(rows,) * 6,
        out_specs=(rows, rows),
        check_vma=False,
    )
```

```python
import functools

import jax
import jax.numpy as jnp
from jax import lax
from jax.experimental import pallas as pl
from jax.experimental.pallas import tpu as pltpu
from jax.sharding import PartitionSpec as P

MESH = pl.DeviceIdType.MESH
K = 4
ITERS = 3
BS = 128
HALF = 8
X, Y, Z = 4, 4, 16
N_DOM = X * Z
GROUP = 4 * Y
SIDE = 64
FAR = range(6, 11)
F32, BF16, I32 = jnp.float32, jnp.bfloat16, jnp.int32


def ring_order(n):
    return sorted(range(1, n), key=lambda d: -min(d, n - d))


def split(v):
    high = v.astype(BF16).astype(F32)
    return jnp.concatenate([high, v - high], axis=0).astype(BF16)


def kernel(
    right_ref, diag_ref, blocks_ref, cols_ref, celld_ref, out_ref,
    rhs, rhs_all, image, image_in, dst, diag_in, dcell, sym, blocks, cols_v, place_s, slot_s, w_off, w_sym,
    mine, win_0, win_1, win_2, prods, spread, tin, red_src, red_a, red_b, red_c, outs,
    local_sems, pair_send, pair_recv, ex_send, ex_recv, red_send, red_recv, meet,
):
    dom, sub = lax.axis_index("dom"), lax.axis_index("sub")
    xx, zz = dom // Z, lax.rem(dom, Z)
    yy, core = sub // 2, lax.rem(sub, 2)
    other = 1 - core
    own = pl.ds(2 * core, 2)
    theirs = pl.ds(2 * other, 2)
    partner = (dom, 2 * yy + other)

    def at(dx, dy, dz):
        return (
            lax.rem(xx + dx, X) * Z + lax.rem(zz + dz, Z),
            2 * lax.rem(yy + dy, Y) + core,
        )

    def dom_at(step, dy):
        return (lax.rem(dom + step + N_DOM, N_DOM), 2 * lax.rem(yy + dy, Y) + core)

    loads = [
        pltpu.make_async_copy(celld_ref, dcell, local_sems.at[0]),
        pltpu.make_async_copy(right_ref.at[:, pl.ds(HALF * core, HALF)], rhs.at[own], local_sems.at[1]),
        pltpu.make_async_copy(diag_ref, diag_in, local_sems.at[2]),
        pltpu.make_async_copy(blocks_ref, blocks.at[own], local_sems.at[3]),
        pltpu.make_async_copy(cols_ref, cols_v.at[core], local_sems.at[4]),
    ]
    loads.append(pltpu.make_async_copy(right_ref, rhs_all, local_sems.at[5]))

    win = (win_0, win_1, win_2)
    for window in win:
        window[...] = jnp.zeros_like(window)
    tin[...] = jnp.zeros_like(tin)

    barrier = pltpu.get_barrier_semaphore()
    plane = [(dx, dy) for dx in range(X) for dy in range(Y) if dx or dy]
    plane.sort(key=lambda p: -(min(p[0], X - p[0]) + min(p[1], Y - p[1])))
    greet = [dom_at(step, dy) for dy in (2, 1, 3, 0) for step in (1, -1)]
    greet += [at(0, 0, dz) for dz in (1, 2, Z - 2, Z - 1)]
    greet += [at(dx, dy, 0) for dx, dy in plane]

    @pl.when(core == 0)
    def _():
        pl.semaphore_signal(barrier, inc=1, device_id=partner, device_id_type=MESH)

    for to_dom, to_sub in greet:
        pl.semaphore_signal(
            barrier, inc=1, device_id=(to_dom, to_sub - core), device_id_type=MESH
        )

    for load in loads:
        load.start()

    def to_partner(index, source, target):
        copy = pltpu.make_async_remote_copy(
            src_ref=source, dst_ref=target, send_sem=pair_send.at[index], recv_sem=pair_recv.at[index],
            device_id=partner, device_id_type=MESH,
        )
        copy.start()
        return copy

    @pl.when(core == 1)
    def _():
        pl.semaphore_wait(barrier, 1)
        pl.semaphore_signal(meet.at[0], inc=1, device_id=partner, device_id_type=MESH)

    @pl.when(core == 0)
    def _():
        pl.semaphore_wait(meet.at[0], 1)

    pair = [
        to_partner(0, right_ref.at[:, pl.ds(HALF * other, HALF)], rhs.at[own]),
        to_partner(2, cols_ref, cols_v.at[core]),
        to_partner(3, blocks_ref, blocks.at[own]),
    ]

    for h in range(4):
        prods[5 * h + K] = jnp.zeros((HALF, BS), F32)
    def tabulate(which):
        base = 2 * which
        columns = cols_v[which]
        places = [columns[i, k] for i in range(2) for k in range(K)]
        places = [jnp.where(place > 0, place, 2 * GROUP) for place in places]
        for i in range(2):
            for k in range(K):
                place_s[(base + i) * K + k] = places[i * K + k]
            for w in range(2 * GROUP):
                slot = K
                for k in range(K):
                    slot = jnp.where(places[i * K + k] == w, k, slot)
                slot_s[(base + i) * 2 * GROUP + w] = slot + (base + i) * (K + 1)

    loads[4].wait()
    tabulate(core)

    def widen(h):
        for k in range(K):
            block = blocks[h, k]
            high = block.astype(BF16)
            w_off[h, 0:BS, k * BS : (k + 1) * BS] = high
            w_off[h, BS : 2 * BS, k * BS : (k + 1) * BS] = (block - high.astype(F32)).astype(BF16)

    def widen_sym(h):
        high = sym[h].astype(BF16)
        w_sym[h, 0:BS, :] = high
        w_sym[h, BS : 2 * BS, :] = (sym[h] - high.astype(F32)).astype(BF16)

    loads[0].wait()
    for i in range(2):
        dst[2 * core + i] = jnp.broadcast_to(dcell[i : i + 1, :], (HALF, BS))
    pair.insert(1, to_partner(1, dst.at[own], dst.at[own]))
    loads[2].wait()
    upper = lax.broadcasted_iota(I32, (BS, BS), 0) < lax.broadcasted_iota(I32, (BS, BS), 1)
    for i in range(2):
        part = jnp.where(upper, diag_in[i], 0.0)
        sym[2 * core + i] = part + part.T
    pair.append(to_partner(4, sym.at[own], sym.at[own]))
    loads[3].wait()
    for i in range(2):
        widen(2 * core + i)
    pair[2].wait_recv()
    tabulate(other)

    @pl.when(core == 0)
    def _():
        pl.semaphore_wait(barrier, 2 * len(greet))
        pl.semaphore_signal(meet.at[0], inc=1, device_id=partner, device_id_type=MESH)

    @pl.when(core == 1)
    def _():
        pl.semaphore_wait(meet.at[0], 1)

    reach = ((1, 2, Z - 2, Z - 1), (4, Z - 4), (6, Z - 6))

    def hail(step):
        for dz in reach[step]:
            pl.semaphore_signal(meet.at[step + 1], inc=1, device_id=at(0, 0, dz), device_id_type=MESH)

    hail(0)

    loads[1].wait()
    pair[0].wait_recv()
    pair[1].wait_recv()
    inverse = [1.0 / dst[h] for h in range(4)]
    u = [[rhs[h] * inverse[h] for h in range(4)]]

    def exchange(index, j, source, target, device):
        return pltpu.make_async_remote_copy(
            src_ref=source, dst_ref=target, send_sem=ex_send.at[j, index], recv_sem=ex_recv.at[j, index],
            device_id=device, device_id_type=MESH,
        )

    def await_bytes(sem, buffer):
        pltpu.make_async_copy(buffer, buffer, sem).wait()

    def send_field_back(j, order):
        @pl.when(dom > 0)
        def _():
            for dy in order:
                exchange(0, j, mine.at[j], win[j].at[pl.ds(GROUP + 4 * yy, 4)], dom_at(-1, dy)).start()

    def send_field_own(j):
        for y_here in range(1, Y):
            @pl.when(yy == y_here)
            def _():
                for y_there in range(y_here):
                    exchange(
                        1, j, mine.at[j], win[j].at[pl.ds(4 * y_here, 4)], (dom, 2 * y_there + core)
                    ).start()

    def send_products_on(j, order):
        @pl.when(dom < N_DOM - 1)
        def _():
            for dy in order:
                rows = pl.ds(GROUP + 4 * lax.rem(yy + dy, Y), 4)
                exchange(2, j, spread.at[j, rows], tin.at[j, Y + yy], dom_at(1, dy)).start()

    def send_products_own(j):
        for y_here in range(Y - 1):
            @pl.when(yy == y_here)
            def _():
                for y_there in range(y_here + 1, Y):
                    exchange(
                        3, j, spread.at[j, pl.ds(4 * y_there, 4)], tin.at[j, y_here], (dom, 2 * y_there + core)
                    ).start()

    def await_field(j):
        for y_here in range(Y - 1):
            @pl.when(yy == y_here)
            def _():
                await_bytes(ex_recv.at[j, 1], win[j].at[pl.ds(0, 4 * (Y - 1 - y_here))])

        @pl.when(dom < N_DOM - 1)
        def _():
            await_bytes(ex_recv.at[j, 0], win[j].at[pl.ds(GROUP, GROUP)])

    def await_products(j):
        for y_here in range(1, Y):
            @pl.when(yy == y_here)
            def _():
                await_bytes(ex_recv.at[j, 3], win[j].at[pl.ds(0, 4 * y_here)])

        @pl.when(dom > 0)
        def _():
            await_bytes(ex_recv.at[j, 2], win[j].at[pl.ds(GROUP, GROUP)])

    def await_sends(j):
        @pl.when(dom > 0)
        def _():
            await_bytes(ex_send.at[j, 0], win[j].at[pl.ds(GROUP, GROUP)])

        @pl.when(dom < N_DOM - 1)
        def _():
            await_bytes(ex_send.at[j, 2], win[j].at[pl.ds(GROUP, GROUP)])

        for y_here in range(Y):
            @pl.when(yy == y_here)
            def _():
                if y_here:
                    await_bytes(ex_send.at[j, 1], win[j].at[pl.ds(0, 4 * y_here)])
                if y_here < Y - 1:
                    await_bytes(ex_send.at[j, 3], win[j].at[pl.ds(0, 4 * (Y - 1 - y_here))])

    def fold(out):
        return (out[0:HALF, 0:BS] + out[0:HALF, BS:]) + (out[HALF:, 0:BS] + out[HALF:, BS:])

    lanes = lax.broadcasted_iota(I32, (HALF, BS), 1)
    sides = lax.broadcasted_iota(I32, (HALF, BS), 0)

    def in_row(first, terms):
        values = jnp.zeros((HALF, BS), F32)
        for index, term in enumerate(terms):
            place = SIDE * core + HALF * (first + index) + sides
            values = jnp.where(lanes == place, jnp.sum(term, axis=1, keepdims=True), values)
        return values

    def swap_image(j, applied):
        for h in range(4):
            image[j, h] = applied[h]
        pair.append(to_partner(5 + j, image.at[j, theirs], image_in.at[j]))

    across = (((1,), (1,)), ((), ()))
    terms = []
    terms.append(sum(rhs[h] * u[0][h] for h in range(4)))

    for j in range(ITERS):
        field = u[j]
        for h in range(4):
            mine[j, h] = field[h]
            win[j][4 * yy + h] = field[h]
        send_field_back(j, (2, 1, 3))
        send_field_own(j)
        send_field_back(j, (0,))
        parts = [split(field[h]) for h in range(4)]
        if j == 0:
            pair[3].wait_recv()
            for i in range(2):
                widen(2 * other + i)
        for h in range(4):
            out = jnp.dot(
                jnp.concatenate([parts[h], parts[h]], axis=1), w_off[h], preferred_element_type=F32
            )
            for k in range(K):
                prods[5 * h + k] = out[0:HALF, k * BS : (k + 1) * BS] + out[HALF:, k * BS : (k + 1) * BS]

        def gather_products(first):
            for w in range(first, first + GROUP):
                picked = [prods[slot_s[h * 2 * GROUP + w]] for h in range(4)]
                spread[j, w] = (picked[0] + picked[1]) + (picked[2] + picked[3])

        gather_products(GROUP)
        send_products_on(j, (2, 1, 3))
        gather_products(0)
        send_products_own(j)
        send_products_on(j, (0,))
        if j == 0:
            pair[4].wait_recv()
            for h in range(4):
                widen_sym(h)
        near = [
            fold(lax.dot_general(parts[h], w_sym[h], across, preferred_element_type=F32)) for h in range(4)
        ]
        if j == ITERS - 1:
            row = in_row(0, terms)
            await_field(j)
            pl.semaphore_wait(meet.at[j + 1], len(reach[j]))
        else:
            pl.semaphore_wait(meet.at[j + 1], len(reach[j]))
            hail(j + 1)
            await_field(j)
        ahead = []
        for h in range(4):
            tiles = [split(win[j][place_s[h * K + k]]) for k in range(K)]
            ahead.append(
                fold(
                    lax.dot_general(
                        jnp.concatenate(tiles, axis=1), w_off[h], across, preferred_element_type=F32
                    )
                )
            )
        if j == ITERS - 1:
            terms.append(sum(field[h] * (2.0 * ahead[h] + near[h]) for h in range(4)))
        else:
            await_products(j)
            applied = []
            for h in range(4):
                back = spread[j, 4 * yy + h]
                for s in range(2 * Y):
                    back = back + tin[j, s, h]
                applied.append(near[h] + ahead[h] + back)
            swap_image(j, applied)
            u.append([applied[h] * inverse[h] for h in range(4)])
            terms.append(sum(field[h] * applied[h] for h in range(4)))
            terms.append(sum(u[j + 1][h] * applied[h] for h in range(4)))

    row = jnp.sum(row + in_row(2 * ITERS - 1, terms[2 * ITERS - 1 :]), axis=0, keepdims=True)
    slot = (zz * Y * X + Y * xx + yy) * 2 + core
    red_a[slot] = row
    red_src[0] = row

    def send_row(source, target, stage, arrival, device):
        pltpu.make_async_remote_copy(
            src_ref=source, dst_ref=target, send_sem=red_send.at[stage], recv_sem=red_recv.at[arrival],
            device_id=device, device_id_type=MESH,
        ).start()

    arrival = jnp.where((zz >= FAR[0]) & (zz <= FAR[-1]), 1, 0)
    for dx, dy in plane:
        to_dom, to_sub = at(dx, dy, Z - zz)
        for to in (to_sub, to_sub + 1 - 2 * core):
            send_row(red_src.at[0], red_a.at[slot], 0, arrival, (to_dom, to))
    to_dom, to_sub = at(0, 0, Z - zz)
    send_row(red_src.at[0], red_a.at[slot], 0, arrival, (to_dom, to_sub + 1 - 2 * core))

    @pl.when(zz > 0)
    def _():
        send_row(red_src.at[0], red_a.at[slot], 0, arrival, (to_dom, to_sub))

    for dx, dy in plane:
        send_row(red_src.at[0], red_a.at[slot], 0, arrival, at(dx, dy, Z + 1 - zz))

    @pl.when(zz != 1)
    def _():
        send_row(red_src.at[0], red_a.at[slot], 0, arrival, at(0, 0, Z + 1 - zz))

    last = ITERS - 1
    await_products(last)
    applied = []
    for h in range(4):
        back = spread[last, 4 * yy + h]
        for s in range(2 * Y):
            back = back + tin[last, s, h]
        applied.append(near[h] + ahead[h] + back)
    swap_image(ITERS - 1, applied)

    near_planes = [z for z in range(Z) if z not in FAR]

    def add_rows(planes, places):
        values = [red_a[2 * X * Y * z + i] for z in planes for i in places]
        while len(values) > 1:
            values = [sum(values[i : i + 2]) for i in range(0, len(values), 2)]
        return values[0]

    @pl.when(zz == 0)
    def _():
        await_bytes(red_recv.at[0], red_a.at[pl.ds(0, 2 * X * Y * len(near_planes) - 1)])
        near_sum = add_rows(near_planes, range(2 * X * Y))
        await_bytes(red_recv.at[1], red_a.at[pl.ds(0, 2 * X * Y * len(FAR))])
        whole = near_sum + add_rows(FAR, range(2 * X * Y))
        red_b[0] = whole
        red_src[1] = whole
        for dz in (2, *range(9, Z)):
            send_row(red_src.at[1], red_b.at[0], 1, 2, at(0, 0, dz))

    @pl.when(zz == 1)
    def _():
        places = [2 * i + core for i in range(X * Y)]
        await_bytes(red_recv.at[0], red_a.at[pl.ds(0, X * Y * len(near_planes) - 1)])
        near_sum = add_rows(near_planes, places)
        await_bytes(red_recv.at[1], red_a.at[pl.ds(0, X * Y * len(FAR))])
        whole = near_sum + add_rows(FAR, places)
        red_src[1] = whole
        swap = pltpu.make_async_remote_copy(
            src_ref=red_src.at[1], dst_ref=red_c.at[0], send_sem=red_send.at[2], recv_sem=red_recv.at[3],
            device_id=partner, device_id_type=MESH,
        )
        swap.start()
        swap.wait_recv()
        whole = whole + red_c[0]
        red_b[0] = whole
        red_src[2] = whole
        for dz in range(2, 8):
            send_row(red_src.at[2], red_b.at[0], 1, 2, at(0, 0, dz))
        swap.wait_send()

    @pl.when(zz > 1)
    def _():
        await_bytes(red_recv.at[2], red_b)

    row = red_b[0]
    lanes = lax.broadcasted_iota(I32, (2 * HALF, BS), 1)
    sides = lax.broadcasted_iota(I32, (2 * HALF, BS), 0)
    first_lane = jnp.where(sides < HALF, SIDE * core + sides, SIDE * other + sides - HALF)
    gram = [
        jnp.broadcast_to(
            jnp.sum(jnp.where(lanes == first_lane + HALF * i, row, 0.0), axis=1, keepdims=True),
            (2 * HALF, BS),
        )
        for i in range(2 * ITERS)
    ]

    def inner(a, b):
        value = None
        for i in range(len(a)):
            for k in range(len(b)):
                if a[i] is not None and b[k] is not None:
                    term = a[i] * b[k] * gram[i + k]
                    value = term if value is None else value + term
        return value

    def plus(a, b):
        return a if b is None else b if a is None else a + b

    one = jnp.ones((2 * HALF, BS), F32)
    zc, pc, xc = [one, None, None, None], [one, None, None], [None, None, None]
    rho = gram[0]
    for step in range(ITERS):
        ac = [pc[0], plus(pc[1], pc[0]), plus(pc[2], pc[1]), pc[2]]
        alpha = rho / inner(pc, ac)
        xc = [plus(xc[i], None if pc[i] is None else alpha * pc[i]) for i in range(3)]
        zc = [plus(zc[i], None if ac[i] is None else -alpha * ac[i]) for i in range(4)]
        if step < ITERS - 1:
            fresh = inner(zc, zc)
            beta = fresh / rho
            pc = [plus(zc[i], None if pc[i] is None else beta * pc[i]) for i in range(3)]
            rho = fresh

    loads[5].wait()
    for copy in pair[5:]:
        copy.wait_recv()
    mine_half, their_half = pl.ds(HALF * core, HALF), pl.ds(HALF * other, HALF)
    for i in range(2):
        h = 2 * core + i
        x, z = [c[:HALF] for c in xc], [c[:HALF] for c in zc]
        outs[0, i, mine_half, :] = x[0] * mine[0, h] + x[1] * mine[1, h] + x[2] * mine[2, h]
        outs[1, i, mine_half, :] = z[0] * rhs[h] + z[1] * image[0, h] + z[2] * image[1, h] + z[3] * image[2, h]
        x, z = [c[HALF:] for c in xc], [c[HALF:] for c in zc]
        right, back = rhs_all[i, their_half, :], 1.0 / dst[h]
        outs[0, i, their_half, :] = (
            x[0] * (right * back) + x[1] * (image_in[0, i] * back) + x[2] * (image_in[1, i] * back)
        )
        outs[1, i, their_half, :] = (
            z[0] * right + z[1] * image_in[0, i] + z[2] * image_in[1, i] + z[3] * image_in[2, i]
        )
    keep = pltpu.make_async_copy(outs, out_ref, local_sems.at[6])
    keep.start()
    for j in range(ITERS):
        await_sends(j)
    await_bytes(red_send.at[0], red_a.at[pl.ds(0, 3 * X * Y - 1)])

    @pl.when(zz > 1)
    def _():
        await_bytes(red_send.at[0], red_b)

    @pl.when(zz == 0)
    def _():
        await_bytes(red_send.at[1], red_a.at[pl.ds(0, 8)])

    @pl.when(zz == 1)
    def _():
        await_bytes(red_send.at[1], red_a.at[pl.ds(0, 6)])

    for copy in pair:
        copy.wait_send()
    keep.wait()


def local(right_side, diag_blocks, block_values, block_cols, block_count, cell_diagonal):
    hbm = pl.BlockSpec(memory_space=pl.ANY)
    both = pl.pallas_call(
        kernel,
        out_shape=jax.ShapeDtypeStruct((2, *right_side.shape), F32),
        in_specs=[hbm] * 5,
        out_specs=hbm,
        scratch_shapes=[
            pltpu.VMEM((4, HALF, BS), F32),
            pltpu.VMEM((2, 2 * HALF, BS), F32),
            pltpu.VMEM((ITERS, 4, HALF, BS), F32),
            pltpu.VMEM((ITERS, 2, HALF, BS), F32),
            pltpu.VMEM((4, HALF, BS), F32),
            pltpu.VMEM((2, BS, BS), F32),
            pltpu.VMEM((2, BS), F32),
            pltpu.VMEM((4, BS, BS), F32),
            pltpu.VMEM((4, K, BS, BS), F32),
            pltpu.VMEM((2, 2, K), I32),
            pltpu.SMEM((4 * K,), I32),
            pltpu.SMEM((4 * 2 * GROUP,), I32),
            pltpu.VMEM((4, 2 * BS, K * BS), BF16),
            pltpu.VMEM((4, 2 * BS, BS), BF16),
            pltpu.VMEM((ITERS, 4, HALF, BS), F32),
            pltpu.VMEM((2 * GROUP + 1, HALF, BS), F32),
            pltpu.VMEM((2 * GROUP + 1, HALF, BS), F32),
            pltpu.VMEM((2 * GROUP + 1, HALF, BS), F32),
            pltpu.VMEM((4 * (K + 1), HALF, BS), F32),
            pltpu.VMEM((ITERS, 2 * GROUP, HALF, BS), F32),
            pltpu.VMEM((ITERS, 2 * Y, 4, HALF, BS), F32),
            pltpu.VMEM((3, 1, BS), F32),
            pltpu.VMEM((2 * X * Y * Z, 1, BS), F32),
            pltpu.VMEM((1, 1, BS), F32),
            pltpu.VMEM((1, 1, BS), F32),
            pltpu.VMEM((2, 2, 2 * HALF, BS), F32),
            pltpu.SemaphoreType.DMA((7,)),
            pltpu.SemaphoreType.DMA((8,)),
            pltpu.SemaphoreType.DMA((8,)),
            pltpu.SemaphoreType.DMA((ITERS, 4)),
            pltpu.SemaphoreType.DMA((ITERS, 4)),
            pltpu.SemaphoreType.DMA((3,)),
            pltpu.SemaphoreType.DMA((4,)),
            pltpu.SemaphoreType.REGULAR((4,)),
        ],
        compiler_params=pltpu.CompilerParams(
            collective_id=0, has_side_effects=True, vmem_limit_bytes=60 << 20
        ),
        name="cg",
    )(right_side, diag_blocks, block_values, block_cols, cell_diagonal)
    return both[0], both[1]


def solution(mesh):
    rows = P(("dom", "sub"))
    return jax.shard_map(
        local,
        mesh=mesh,
        in_specs=(rows,) * 6,
        out_specs=(rows, rows),
        check_vma=False,
    )
```
